32 devices in a mesh: case: 2 (over x), wide: 16 (over z, y, core).
Axes of the slice: x: 2, y: 2, z: 4, core: 2. Of those that a mesh axis runs over, the one named last changes fastest.
Arguments:
- flow: bfloat16 [5, 16, 65536], P(None, None, ('case', 'wide')), parts along dimension 2, may hold values from -6 to 6
- positions: bfloat16 [3, 65536], P(None, ('case', 'wide')), parts along dimension 1, may hold values from -1.1953125 to 1.1953125
- normals: bfloat16 [3, 65536], P(None, ('case', 'wide')), parts along dimension 1, may hold values from -6 to 6
- panel_ids: int32 [65536], P(('case', 'wide')), parts along dimension 0, may hold values from 0 to 32767, as said below
- observers: float32 [2, 512], P(None, ('case', 'wide')), parts along dimension 1, may hold values from -6 to 6
Outputs:
- panel_spectra: bfloat16 [32, 65536], P(None, ('case', 'wide')), parts along dimension 1
- pressure: float32 [512, 8], P(('case', 'wide')), parts along dimension 0
The draws below stay inside these ranges and needn't reach their ends.
There are 2 independent parts, one for each index of `case`. The reference program is written for one: setup_inputs(seed, part) draws one part's arguments, and reference() takes and returns one part's arrays. A program takes and returns all parts, laid end to end along the dimension named above; each array names one. Nothing has to cross between parts.
Inputs may be any that keep to these rules, and one draw needn't show every extreme that they name: `panel_ids`: every number 0 to 32767 appears exactly once; panel g belongs to device g // 2048 of wide at local position g % 2048, so every device owns exactly 2048 panels. The 2048 columns of one device name each owner at most 256 times, and every device names some owner exactly 256 times.
All inputs are finite; a program needn't handle non-finite values.
Results may differ from the reference program's by a relative error of at most 0.0034.
Values may be sent and summed in bfloat16 or wider, within the bound.
No kernel may reach another device: no remote copies, remote signals or barrier semaphores. Data moves between devices by JAX's collectives and lax.ppermute only.
A program may use at most 192 MiB of HBM per device.

```python
import math
import jax
import jax.numpy as jnp
from jax import lax

NT = 16
HARM = 4
PAN_DEV = 2048
PANELS = 32768
OBS = 256
CAP = 256


def draw_panel_ids(key, part):
    nwide = PANELS // PAN_DEV
    half = nwide // 2
    keys = jax.random.split(key, 6)
    extra = jax.random.randint(keys[0], (half - 1,), 0, CAP + 1).astype(jnp.int32)
    weights = jnp.concatenate([jnp.array([CAP, 0], jnp.int32), jnp.stack([extra, CAP - extra], axis=1).reshape(-1)])
    weights = jax.random.permutation(keys[1], weights)
    sigma = jax.random.permutation(keys[2], nwide)
    tau = jax.random.permutation(keys[3], nwide)
    counts = weights[(tau[None, :] - sigma[:, None]) % nwide]
    offsets = jnp.cumsum(counts, axis=0) - counts
    ends = jnp.cumsum(counts, axis=1)
    position = jnp.arange(PAN_DEV, dtype=jnp.int32)
    owner = jnp.sum((ends[:, None, :] <= position[None, :, None]).astype(jnp.int32), axis=2)
    begins = jnp.take_along_axis(ends - counts, owner, axis=1)
    local = jnp.take_along_axis(offsets, owner, axis=1) + position[None, :] - begins
    shuffle = jax.vmap(lambda item: jax.random.permutation(item, PAN_DEV))(jax.random.split(keys[4], nwide))
    mapped = shuffle[owner, local]
    ids = owner * PAN_DEV + mapped
    order = jax.vmap(lambda item: jax.random.permutation(item, PAN_DEV))(jax.random.split(keys[5], nwide))
    ids = jnp.take_along_axis(ids, order, axis=1)
    return ids.reshape(-1).astype(jnp.int32)


def block_levels(rng, dims, pieces, low, high):
    loudness, own = 1.0, jax.random.fold_in(rng, 6)
    for dim, blocks in pieces:
        heights = jnp.exp(jax.random.uniform(jax.random.fold_in(own, dim), (blocks,), jnp.float32, low / len(pieces), high / len(pieces)))
        loudness = loudness * jnp.repeat(heights, dims[dim] // blocks).reshape([-1 if axis == dim else 1 for axis in range(len(dims))])
    return loudness


def scatter_about(own_key, shape, spread, most, pieces=(), kind=jnp.bfloat16):
    entries = spread * jax.random.normal(own_key, shape, jnp.float32)
    if pieces:
        entries = entries * block_levels(own_key, shape, pieces, -0.22, 0.18)
    return jnp.clip(entries, -most, most).astype(kind)


def setup_inputs(seed: int = 0, part: int = 0) -> dict:
    splits = jax.random.split(jax.random.key(seed), 6)
    part_keys = jax.random.split(jax.random.fold_in(splits[5], part), 6)
    flow = scatter_about(part_keys[0], (5, NT, PANELS), 1.0, 6.0, ((2, 16),))
    positions = jnp.clip(jax.random.uniform(part_keys[1], (3, PANELS), jnp.float32, -1.1953125, 1.1953125) * block_levels(part_keys[1], (3, PANELS), ((1, 16),), -0.4, 0.0), -1.1953125, 1.1953125).astype(jnp.bfloat16)
    normals = scatter_about(part_keys[2], (3, PANELS), 1.0, 6.0, ((1, 16),))
    panel_ids = draw_panel_ids(jax.random.fold_in(jax.random.fold_in(splits[5], part), 71), part)
    observers = jnp.clip(jax.random.uniform(part_keys[4], (2, OBS), jnp.float32, -6.0, 6.0) * block_levels(part_keys[4], (2, OBS), ((1, 16),), -0.4, 0.0), -6.0, 6.0)
    return dict(flow=flow, positions=positions, normals=normals, panel_ids=panel_ids, observers=observers)


WAVENUMBER = 2.0
GROUND = 3.0

def dft_table():
    samples = jnp.arange(NT, dtype=jnp.float32)[:, None]
    harmonic = jnp.arange(1, HARM + 1, dtype=jnp.float32)[None, :]
    angle = 2.0 * math.pi / NT * samples * harmonic
    table = jnp.stack([jnp.cos(angle), -jnp.sin(angle)], axis=2) * (2.0 / NT)
    return table.reshape(NT, 2 * HARM)

def spectra_of(flow, normals):
    values = flow.astype(jnp.float32)
    normal_vec = normals.astype(jnp.float32)[:, None, :]
    density = 1.0 + 0.2 * values[0]
    velocity = 0.5 * values[1:4]
    fluctuation = values[4]
    normal_vel = lax.optimization_barrier(jnp.sum(velocity * normal_vec, axis=0))
    source = density * normal_vel
    loads = fluctuation[None] * normal_vec + density[None] * velocity * normal_vel[None]
    quantities = jnp.concatenate([source[None], loads], axis=0)
    spectra = jnp.einsum('qtp,tc->qcp', quantities, dft_table(), precision=lax.Precision.HIGHEST)
    return spectra.reshape(8 * HARM, -1).astype(jnp.bfloat16)

def pressure_sums(spectra, positions, listeners):
    parts = spectra.astype(jnp.float32).reshape(4, HARM, 2, -1)
    place = positions.astype(jnp.float32)
    delta_x = listeners[0][:, None] - place[0][None, :]
    delta_y = listeners[1][:, None] - place[1][None, :]
    delta_z = -GROUND - place[2][None, :]
    distance = jnp.sqrt(delta_x * delta_x + delta_y * delta_y + delta_z * delta_z)
    inverse = 1.0 / distance
    unit_x = delta_x * inverse
    unit_y = delta_y * inverse
    unit_z = delta_z * inverse
    columns = []
    for harmonic in range(HARM):
        wavenum = WAVENUMBER * (harmonic + 1)
        source_re = parts[0, harmonic, 0][None, :]
        source_im = parts[0, harmonic, 1][None, :]
        along_re = parts[1, harmonic, 0][None, :] * unit_x + parts[2, harmonic, 0][None, :] * unit_y + parts[3, harmonic, 0][None, :] * unit_z
        along_im = parts[1, harmonic, 1][None, :] * unit_x + parts[2, harmonic, 1][None, :] * unit_y + parts[3, harmonic, 1][None, :] * unit_z
        bracket_re = -wavenum * source_im + along_re * inverse - wavenum * along_im
        bracket_im = wavenum * source_re + along_im * inverse + wavenum * along_re
        phase = wavenum * distance
        cosine = jnp.cos(phase)
        sine = jnp.sin(phase)
        columns.append(lax.optimization_barrier(jnp.sum((cosine * bracket_re + sine * bracket_im) * inverse, axis=1)))
        columns.append(lax.optimization_barrier(jnp.sum((cosine * bracket_im - sine * bracket_re) * inverse, axis=1)))
    return jnp.stack(columns, axis=1)

def reference(flow, positions, normals, panel_ids, observers):
    spectra = spectra_of(flow, normals)
    panel_spectra = jnp.zeros_like(spectra).at[:, panel_ids].set(spectra)
    blocks = observers.reshape(2, OBS // 8, 8).transpose(1, 0, 2)
    sums = lax.map(lambda block: pressure_sums(spectra, positions, block), blocks)
    pressure = sums.reshape(OBS, 2 * HARM) * (2.0 / math.sqrt(PANELS))
    return (panel_spectra, pressure)
```

```python
import math

import jax
import jax.numpy as jnp
import numpy as np
from jax import lax
from jax.experimental import pallas as pl
from jax.experimental.pallas import tpu as pltpu
from jax.sharding import PartitionSpec as P

NT = 16
HARM = 4
ROWS = 8 * HARM
WAVENUMBER = 2.0
GROUND = 3.0
LOW = 256
F32 = jnp.float32
BF16 = jnp.bfloat16
NT_DIMS = (((1,), (1,)), ((), ()))


def dft_split():
    samples = np.arange(NT)[:, None]
    harmonic = np.arange(1, HARM + 1)[None, :]
    angle = 2.0 * np.pi / NT * samples * harmonic
    table = np.stack([np.cos(angle), -np.sin(angle)], axis=2) * (2.0 / NT)
    table = table.reshape(NT, 2 * HARM).T
    block = np.kron(np.eye(4), table).astype(np.float32)
    high = block.astype(jnp.bfloat16)
    low = (block - high.astype(np.float32)).astype(jnp.bfloat16)
    return np.concatenate([high, high, low, low], axis=1)


def pack_shape(nwide, owned):
    capacity = 2 * owned // nwide
    lanes = min(capacity, 128)
    subs = capacity // lanes
    return capacity, lanes, subs, ROWS * subs + 16


def source_kernel(nwide, flow_ref, normals_ref, ids_ref, table_ref, spectra_ref, packed_ref, left, right):
    owned = flow_ref.shape[2]
    capacity, lanes, subs, _ = pack_shape(nwide, owned)
    step = min(256, owned)
    table = table_ref[...]
    upper = (
        lax.broadcasted_iota(jnp.int32, (step, step), 0)
        < lax.broadcasted_iota(jnp.int32, (step, step), 1)
    ).astype(F32).astype(BF16)
    ids = ids_ref[...]
    owner = ids // owned
    local = ids - owner * owned
    high = local // LOW
    code_high = (high + 1).astype(F32)
    code_low = (local - high * LOW).astype(F32)
    carry = jnp.zeros((nwide, 1), F32)
    which = lax.broadcasted_iota(jnp.int32, (nwide, step), 0)
    slots = lax.broadcasted_iota(jnp.int32, (capacity, step), 0).astype(F32)
    codes_row = lax.broadcasted_iota(jnp.int32, (8, step), 0)
    for start in range(0, owned, step):
        cols = slice(start, start + step)
        normal = normals_ref[:, cols].astype(F32)
        n0, n1, n2 = normal[0:1], normal[1:2], normal[2:3]
        density = 1.0 + 0.2 * flow_ref[0, :, cols].astype(F32)
        v0 = 0.5 * flow_ref[1, :, cols].astype(F32)
        v1 = 0.5 * flow_ref[2, :, cols].astype(F32)
        v2 = 0.5 * flow_ref[3, :, cols].astype(F32)
        fluct = flow_ref[4, :, cols].astype(F32)
        across = v0 * n0 + v1 * n1 + v2 * n2
        source = density * across
        parts = jnp.concatenate(
            [source, fluct * n0 + v0 * source, fluct * n1 + v1 * source, fluct * n2 + v2 * source], axis=0
        )
        top = parts.astype(BF16)
        rest = (parts - top.astype(F32)).astype(BF16)
        both = jnp.concatenate([top, rest, top, rest], axis=0)
        spectra = jnp.dot(table, both, preferred_element_type=F32).astype(BF16)
        spectra_ref[:, cols] = spectra

        own = which == owner[:, cols]
        ownf = own.astype(F32)
        before = jnp.dot(ownf.astype(BF16), upper, preferred_element_type=F32) + carry
        rank = jnp.sum(before * ownf, axis=0, keepdims=True)
        carry = before[:, step - 1 : step] + ownf[:, step - 1 : step]
        right[:, cols] = (slots == rank).astype(F32).astype(BF16)
        codes = jnp.where(codes_row == 0, code_high[:, cols], jnp.where(codes_row == 1, code_low[:, cols], 0.0))
        codes = jnp.concatenate([codes, jnp.zeros_like(codes)], axis=0).astype(BF16)
        values = jnp.concatenate([spectra, codes], axis=0)
        for o in range(nwide):
            left[48 * o : 48 * o + 48, cols] = jnp.where(owner[:, cols] == o, values, jnp.zeros_like(values))
    packed = lax.dot_general(left[...], right[...], NT_DIMS, preferred_element_type=F32)
    for o in range(nwide):
        block = packed[48 * o : 48 * o + 48]
        pieces = [block[:ROWS, lanes * s : lanes * s + lanes] for s in range(subs)]
        pieces += [block[ROWS : ROWS + 8, lanes * s : lanes * s + lanes] for s in range(subs)]
        if subs == 1:
            pieces.append(jnp.zeros((8, lanes), F32))
        packed_ref[o] = jnp.concatenate(pieces, axis=0).astype(BF16)


def sources(flow, normals, ids, nwide):
    owned = flow.shape[2]
    capacity, lanes, subs, depth = pack_shape(nwide, owned)
    vmem = pl.BlockSpec(memory_space=pltpu.VMEM)
    table = jnp.asarray(dft_split())

    def body(*refs):
        source_kernel(nwide, *refs)

    return pl.pallas_call(
        body,
        out_shape=(
            jax.ShapeDtypeStruct((ROWS, owned), BF16),
            jax.ShapeDtypeStruct((nwide, depth, lanes), BF16),
        ),
        in_specs=[vmem] * 4,
        out_specs=(vmem, vmem),
        scratch_shapes=[
            pltpu.VMEM((48 * nwide, owned), BF16),
            pltpu.VMEM((capacity, owned), BF16),
        ],
        compiler_params=pltpu.CompilerParams(vmem_limit_bytes=48 * 2**20),
    )(flow, normals, ids.reshape(1, owned), table)


def place_kernel(received_ref, spectra_ref):
    nwide, depth, lanes = received_ref.shape
    owned = spectra_ref.shape[1]
    subs = (depth - 16) // ROWS
    heights = owned // LOW
    group = max(1, 256 // (lanes * subs))
    width = lanes * subs * group
    lows = lax.broadcasted_iota(jnp.int32, (LOW, width), 0).astype(F32)
    total = jnp.zeros((heights * ROWS, LOW), F32)
    for first in range(0, nwide, group):
        blocks, high, low = [], [], []
        for o in range(first, first + group):
            codes = received_ref[o, ROWS * subs : ROWS * subs + 16, :].astype(F32)
            for s in range(subs):
                blocks.append(received_ref[o, ROWS * s : ROWS * s + ROWS, :])
                high.append(codes[8 * s : 8 * s + 1])
                low.append(codes[8 * s + 1 : 8 * s + 2])
        values = jnp.concatenate(blocks, axis=1)
        high = jnp.concatenate(high, axis=1)
        low = jnp.concatenate(low, axis=1)
        spread = (lows == low).astype(F32).astype(BF16)
        picked = jnp.concatenate(
            [jnp.where(high == h + 1.0, values, jnp.zeros_like(values)) for h in range(heights)], axis=0
        )
        total = total + lax.dot_general(picked, spread, NT_DIMS, preferred_element_type=F32)
    for h in range(heights):
        spectra_ref[:, LOW * h : LOW * h + LOW] = total[ROWS * h : ROWS * h + ROWS].astype(BF16)


def place(received, owned):
    vmem = pl.BlockSpec(memory_space=pltpu.VMEM)
    return pl.pallas_call(
        place_kernel,
        out_shape=jax.ShapeDtypeStruct((ROWS, owned), BF16),
        in_specs=[vmem],
        out_specs=vmem,
        compiler_params=pltpu.CompilerParams(vmem_limit_bytes=48 * 2**20),
    )(received)


def fit(function, degree):
    nodes = np.cos(np.pi * (np.arange(64) + 0.5) / 64) * 0.5
    squares = nodes * nodes
    powers = np.stack([squares**d for d in range(degree + 1)], axis=1)
    return [float(c) for c in np.linalg.lstsq(powers, function(nodes), rcond=None)[0]]


COS = fit(lambda f: 2.0 * np.cos(2.0 * np.pi * f), 5)
SIN = fit(lambda f: np.sin(2.0 * np.pi * f) / f, 4)


def horner(coefficients, x):
    value = coefficients[-1]
    for c in coefficients[-2::-1]:
        value = value * x + c
    return value


KINDS = 4
COLS = 16


def sums_kernel(spectra_ref, place_ref, over_ref, sums_ref, weights):
    owned = spectra_ref.shape[1]
    count = over_ref.shape[0]
    step = min(256, owned)
    tile = 64
    steps = owned // step

    place_all = place_ref[...].astype(F32)
    px, py, pz = place_all[0:1], place_all[1:2], place_all[2:3]
    for h in range(HARM):
        def row(a, c):
            r = 2 * HARM * a + 2 * h + c
            return spectra_ref[r : r + 1, :].astype(F32)

        qr, qi = row(0, 0), row(0, 1)
        xr, xi, yr, yi, zr, zi = row(1, 0), row(1, 1), row(2, 0), row(2, 1), row(3, 0), row(3, 1)
        tr = -GROUND * zr - (px * xr + py * yr + pz * zr)
        ti = -GROUND * zi - (px * xi + py * yi + pz * zi)
        trh = tr.astype(BF16).astype(F32)
        tih = ti.astype(BF16).astype(F32)
        trl, til = tr - trh, ti - tih
        zero = jnp.zeros_like(qr)
        six = [zero] * 6
        blocks = [
            [-qi, qr] + [zero] * 8,
            [qr, qi] + [zero] * 8,
            [zero, zero, trh, tih, trl, til, xr, xi, yr, yi],
            [zero, zero, -tih, trh, -til, trl, -xi, xr, -yi, yr],
        ]
        for kind, rows in enumerate(blocks):
            value = jnp.concatenate(rows + [zero] * (COLS - len(rows)), axis=0).astype(BF16)
            for i in range(steps):
                weights[i, h, :, kind * step : kind * step + step] = value[:, i * step : i * step + step]

    for o in range(0, count, tile):
        ox = over_ref[o : o + tile, 0:1]
        oy = over_ref[o : o + tile, 1:2]
        ox2, oy2 = -2.0 * ox, -2.0 * oy
        oc = ox * ox + oy * oy + GROUND * GROUND
        acc = [jnp.zeros((tile, COLS), F32) for _ in range(HARM)]
        for i in range(steps):
            cols = slice(i * step, i * step + step)
            pxs, pys, pzs = px[:, cols], py[:, cols], pz[:, cols]
            pc = pxs * pxs + pys * pys + pzs * pzs + (2.0 * GROUND) * pzs
            square = (oc + pc) + ox2 * pxs + oy2 * pys
            inv = lax.rsqrt(square)
            turns = (square * inv) * (WAVENUMBER / (2.0 * math.pi))
            frac = turns - jnp.round(turns)
            fsq = frac * frac
            twoc = horner(COS, fsq)
            sine = horner(SIN, fsq) * frac
            c_prev, s_prev = inv, None
            c_now, s_now = (0.5 * inv) * twoc, inv * sine
            for h in range(HARM):
                wavenum = WAVENUMBER * (h + 1)
                ratio = inv * (1.0 / wavenum)
                d, e = inv * c_now, inv * s_now
                g_re = ratio * d + e
                g_im = d - ratio * e
                g = jnp.concatenate(
                    [c_now.astype(BF16), s_now.astype(BF16), g_re.astype(BF16), g_im.astype(BF16)], axis=1
                )
                acc[h] = acc[h] + lax.dot_general(g, weights[i, h], NT_DIMS, preferred_element_type=F32)
                if h < HARM - 1:
                    c_next = twoc * c_now - c_prev
                    s_next = twoc * s_now - s_prev if h else twoc * s_now
                    c_prev, s_prev, c_now, s_now = c_now, s_now, c_next, s_next
        outs = []
        for h in range(HARM):
            wavenum = WAVENUMBER * (h + 1)
            a = acc[h]
            for c in range(2):
                outs.append(
                    wavenum
                    * (a[:, c : c + 1] + a[:, 2 + c : 3 + c] + a[:, 4 + c : 5 + c] + ox * a[:, 6 + c : 7 + c] + oy * a[:, 8 + c : 9 + c])
                )
        sums_ref[o : o + tile, :] = jnp.concatenate(outs, axis=1)


def pressure_sums(spectra, positions, over):
    owned = spectra.shape[1]
    count = over.shape[0]
    step = min(256, owned)
    vmem = pl.BlockSpec(memory_space=pltpu.VMEM)
    return pl.pallas_call(
        sums_kernel,
        out_shape=jax.ShapeDtypeStruct((count, 2 * HARM), F32),
        in_specs=[vmem] * 3,
        out_specs=vmem,
        scratch_shapes=[pltpu.VMEM((owned // step, HARM, COLS, KINDS * step), BF16)],
        compiler_params=pltpu.CompilerParams(vmem_limit_bytes=48 * 2**20),
    )(spectra, positions, over)


def shards(flow, positions, normals, panel_ids, observers):
    owned = flow.shape[2]
    nwide = lax.axis_size("wide")
    listeners = observers.shape[1]
    mine = jnp.broadcast_to(observers.T[None], (nwide, listeners, 2))
    over = lax.all_to_all(mine, "wide", split_axis=0, concat_axis=0, tiled=True)
    spectra, packed = sources(flow, normals, panel_ids, nwide)
    received = lax.all_to_all(packed, "wide", split_axis=0, concat_axis=0, tiled=True)
    sums = pressure_sums(spectra, positions, over.reshape(nwide * listeners, 2))
    shares = lax.all_to_all(
        sums.reshape(nwide, listeners, 2 * HARM), "wide", split_axis=0, concat_axis=0, tiled=True
    )
    panel_spectra = place(received, owned)
    pressure = jnp.sum(shares, axis=0) * (2.0 / math.sqrt(owned * nwide))
    return (panel_spectra, pressure)


def solution(mesh):
    placed = (
        P(None, None, ("case", "wide")),
        P(None, ("case", "wide")),
        P(None, ("case", "wide")),
        P(("case", "wide")),
        P(None, ("case", "wide")),
    )
    return jax.shard_map(
        shards,
        mesh=mesh,
        in_specs=placed,
        out_specs=(P(None, ("case", "wide")), P(("case", "wide"), None)),
        check_vma=False,
    )
```

```python
import math

import jax
import jax.numpy as jnp
import numpy as np
from jax import lax
from jax.experimental import pallas as pl
from jax.experimental.pallas import tpu as pltpu
from jax.sharding import PartitionSpec as P

NT = 16
HARM = 4
ROWS = 8 * HARM
WAVENUMBER = 2.0
GROUND = 3.0
LOW = 256
F32 = jnp.float32
BF16 = jnp.bfloat16
NT_DIMS = (((1,), (1,)), ((), ()))


def fit(function, degree):
    nodes = np.cos(np.pi * (np.arange(64) + 0.5) / 64) * 0.5
    squares = nodes * nodes
    powers = np.stack([squares**d for d in range(degree + 1)], axis=1)
    return [float(c) for c in np.linalg.lstsq(powers, function(nodes), rcond=None)[0]]


TURN = WAVENUMBER / (2.0 * math.pi)
HALF_SINE = fit(lambda f: math.sqrt(2.0) * np.sin(np.pi * f) / f, 4)


def horner(coefficients, x):
    value = coefficients[-1]
    for c in coefficients[-2::-1]:
        value = value * x + c
    return value


def thirds(x):
    first = x.astype(BF16).astype(F32)
    second = (x - first).astype(BF16).astype(F32)
    return [first, second, x - first - second]


def dft_split():
    samples = np.arange(NT)[:, None]
    harmonic = np.arange(1, HARM + 1)[None, :]
    angle = 2.0 * np.pi / NT * samples * harmonic
    table = np.stack([np.cos(angle), -np.sin(angle)], axis=2) * (2.0 / NT)
    table = table.reshape(NT, 2 * HARM).T
    block = np.kron(np.eye(4), table).astype(np.float32)
    order = [8 * a + 2 * h + c for h in range(HARM) for a in range(4) for c in range(2)]
    block = np.concatenate([block, block[order]], axis=0)
    high = block.astype(jnp.bfloat16)
    low = (block - high.astype(np.float32)).astype(jnp.bfloat16)
    return np.concatenate([high, high, low, low], axis=1)


def pack_shape(nwide, owned):
    capacity = 2 * owned // nwide
    lanes = min(capacity, 128)
    subs = capacity // lanes
    return capacity, lanes, subs, ROWS * subs + 16


def source_kernel(
    flow_hbm, normals_hbm, place_hbm, table_hbm, spectra_ref, weights_ref, points_ref,
    flow_ref, normals_ref, place_ref, table_ref, sems,
):
    owned = flow_ref.shape[2]
    step = min(256, owned)
    pieces = 4
    wide = owned // pieces
    copies = [
        pltpu.make_async_copy(normals_hbm, normals_ref, sems.at[0]),
        pltpu.make_async_copy(place_hbm, place_ref, sems.at[1]),
        pltpu.make_async_copy(table_hbm, table_ref, sems.at[2]),
    ]
    flows = [
        pltpu.make_async_copy(
            flow_hbm.at[:, :, wide * p : wide * p + wide], flow_ref.at[:, :, wide * p : wide * p + wide], sems.at[3 + p]
        )
        for p in range(pieces)
    ]
    for copy in copies + flows:
        copy.start()
    for copy in copies:
        copy.wait()
    table = table_ref[...]
    scale = TURN * TURN
    for start in range(0, owned, step):
        if start % wide == 0:
            flows[start // wide].wait()
        cols = slice(start, start + step)
        normal = normals_ref[:, cols].astype(F32)
        n0, n1, n2 = normal[0:1], normal[1:2], normal[2:3]
        density = 1.0 + 0.2 * flow_ref[0, :, cols].astype(F32)
        v0 = 0.5 * flow_ref[1, :, cols].astype(F32)
        v1 = 0.5 * flow_ref[2, :, cols].astype(F32)
        v2 = 0.5 * flow_ref[3, :, cols].astype(F32)
        fluct = flow_ref[4, :, cols].astype(F32)
        across = v0 * n0 + v1 * n1 + v2 * n2
        source = density * across
        parts = jnp.concatenate(
            [source, fluct * n0 + v0 * source, fluct * n1 + v1 * source, fluct * n2 + v2 * source], axis=0
        )
        top = parts.astype(BF16)
        rest = (parts - top.astype(F32)).astype(BF16)
        both = jnp.concatenate([top, rest, top, rest], axis=0)
        spectra = jnp.dot(table, both, preferred_element_type=F32).astype(BF16)
        spectra_ref[:, cols] = spectra[:ROWS]
        by_harmonic = spectra[ROWS:].astype(F32)
        place = place_ref[:, cols].astype(F32)
        px, py, pz = place[0:1], place[1:2], place[2:3]
        down = pz + GROUND
        none = jnp.zeros_like(px)
        factors = jnp.concatenate([none, none, px, px, py, py, down, down], axis=0)
        for h in range(HARM):
            group = by_harmonic[8 * h : 8 * h + 8]
            shares = group * factors
            along = -(shares[2:4] + shares[4:6] + shares[6:8])
            along_high = along.astype(BF16).astype(F32)
            weights_ref[h, :, cols] = jnp.concatenate(
                [group, along_high, along - along_high, jnp.zeros((4, step), F32)], axis=0
            ).astype(BF16)
        here = scale * (px * px + py * py + pz * pz + (2.0 * GROUND) * pz)
        one = jnp.ones_like(here)
        points = jnp.concatenate([px] * 3 + [py] * 3 + [one] * 3 + thirds(here) + [none] * 4, axis=0)
        points_ref[cols, :] = points.T.astype(BF16)


def sources(flow, normals, positions):
    owned = flow.shape[2]
    vmem = pl.BlockSpec(memory_space=pltpu.VMEM)
    anywhere = pl.BlockSpec(memory_space=pl.ANY)
    table = jnp.asarray(dft_split())
    return pl.pallas_call(
        source_kernel,
        out_shape=(
            jax.ShapeDtypeStruct((ROWS, owned), BF16),
            jax.ShapeDtypeStruct((HARM, 16, owned), BF16),
            jax.ShapeDtypeStruct((owned, 16), BF16),
        ),
        in_specs=[anywhere] * 4,
        out_specs=(vmem,) * 3,
        scratch_shapes=[
            pltpu.VMEM(flow.shape, BF16),
            pltpu.VMEM(normals.shape, BF16),
            pltpu.VMEM(positions.shape, BF16),
            pltpu.VMEM(table.shape, BF16),
            pltpu.SemaphoreType.DMA((7,)),
        ],
        compiler_params=pltpu.CompilerParams(vmem_limit_bytes=32 * 2**20),
    )(flow, normals, positions, table)


def pack_kernel(nwide, spectra_ref, ids_ref, packed_ref, codes_ref, left, right):
    owned = spectra_ref.shape[1]
    capacity, lanes, subs, _ = pack_shape(nwide, owned)
    step = min(256, owned)
    upper = (
        lax.broadcasted_iota(jnp.int32, (step, step), 0)
        < lax.broadcasted_iota(jnp.int32, (step, step), 1)
    ).astype(F32).astype(BF16)
    ids = ids_ref[...]
    owner = ids // owned
    local = ids - owner * owned
    high = local // LOW
    code_high = (high + 1).astype(F32)
    code_low = (local - high * LOW).astype(F32)
    carry = jnp.zeros((nwide, 1), F32)
    which = lax.broadcasted_iota(jnp.int32, (nwide, step), 0)
    slots = lax.broadcasted_iota(jnp.int32, (capacity, step), 0).astype(F32)
    codes_row = lax.broadcasted_iota(jnp.int32, (8, step), 0)
    for start in range(0, owned, step):
        cols = slice(start, start + step)
        own = which == owner[:, cols]
        ownf = own.astype(F32)
        before = jnp.dot(ownf.astype(BF16), upper, preferred_element_type=F32) + carry
        rank = jnp.sum(before * ownf, axis=0, keepdims=True)
        carry = before[:, step - 1 : step] + ownf[:, step - 1 : step]
        right[:, cols] = (slots == rank).astype(F32).astype(BF16)
        codes = jnp.where(codes_row == 0, code_high[:, cols], jnp.where(codes_row == 1, code_low[:, cols], 0.0))
        codes = jnp.concatenate([codes, jnp.zeros_like(codes)], axis=0).astype(BF16)
        values = jnp.concatenate([spectra_ref[:, cols], codes], axis=0)
        for o in range(nwide):
            left[48 * o : 48 * o + 48, cols] = jnp.where(owner[:, cols] == o, values, jnp.zeros_like(values))
    packed = lax.dot_general(left[...], right[...], NT_DIMS, preferred_element_type=F32)
    for o in range(nwide):
        block = packed[48 * o : 48 * o + 48]
        for s in range(subs):
            packed_ref[o, ROWS * s : ROWS * s + ROWS, :] = block[:ROWS, lanes * s : lanes * s + lanes].astype(BF16)
        codes = [block[ROWS : ROWS + 2, lanes * s : lanes * s + lanes] for s in range(subs)]
        codes_ref[o] = jnp.concatenate(codes + [jnp.zeros((8 - 2 * subs, lanes), F32)], axis=0)


def pack(spectra, ids, nwide):
    owned = spectra.shape[1]
    capacity, lanes, subs, depth = pack_shape(nwide, owned)
    vmem = pl.BlockSpec(memory_space=pltpu.VMEM)

    def body(*refs):
        pack_kernel(nwide, *refs)

    return pl.pallas_call(
        body,
        out_shape=(
            jax.ShapeDtypeStruct((nwide, depth, lanes), BF16),
            jax.ShapeDtypeStruct((nwide, 8, lanes), F32),
        ),
        in_specs=[vmem] * 2,
        out_specs=(vmem, vmem),
        scratch_shapes=[
            pltpu.VMEM((48 * nwide, owned), BF16),
            pltpu.VMEM((capacity, owned), BF16),
        ],
        compiler_params=pltpu.CompilerParams(vmem_limit_bytes=40 * 2**20),
    )(spectra, ids.reshape(1, owned))


def place_kernel(scale, received_ref, spectra_ref, pressure_ref):
    nwide, depth, lanes = received_ref.shape
    owned = spectra_ref.shape[1]
    listeners = pressure_ref.shape[1]
    subs = (depth - 16) // ROWS
    heights = owned // LOW
    group = max(1, 256 // (lanes * subs))
    width = lanes * subs * group
    lows = lax.broadcasted_iota(jnp.int32, (LOW, width), 0).astype(F32)
    total = jnp.zeros((heights * ROWS, LOW), F32)
    sums = jnp.zeros((2 * HARM, lanes), F32)
    for first in range(0, nwide, group):
        blocks, high, low = [], [], []
        for o in range(first, first + group):
            codes = received_ref[o, ROWS * subs : ROWS * subs + 16, :].astype(F32)
            sums = sums + codes[8:16]
            for s in range(subs):
                blocks.append(received_ref[o, ROWS * s : ROWS * s + ROWS, :])
                high.append(codes[2 * s : 2 * s + 1])
                low.append(codes[2 * s + 1 : 2 * s + 2])
        values = jnp.concatenate(blocks, axis=1)
        high = jnp.concatenate(high, axis=1)
        low = jnp.concatenate(low, axis=1)
        spread = (lows == low).astype(F32).astype(BF16)
        picked = jnp.concatenate(
            [jnp.where(high == h + 1.0, values, jnp.zeros_like(values)) for h in range(heights)], axis=0
        )
        total = total + lax.dot_general(picked, spread, NT_DIMS, preferred_element_type=F32)
    for h in range(heights):
        spectra_ref[:, LOW * h : LOW * h + LOW] = total[ROWS * h : ROWS * h + ROWS].astype(BF16)
    third = [sums[:, listeners * p : listeners * p + listeners] for p in range(3)]
    pressure_ref[...] = scale * ((third[2] + third[1]) + third[0])


def place(received, owned, listeners):
    nwide = received.shape[0]
    vmem = pl.BlockSpec(memory_space=pltpu.VMEM)
    scale = 2.0 / math.sqrt(owned * nwide)

    def body(*refs):
        place_kernel(scale, *refs)

    return pl.pallas_call(
        body,
        out_shape=(
            jax.ShapeDtypeStruct((ROWS, owned), BF16),
            jax.ShapeDtypeStruct((2 * HARM, listeners), F32),
        ),
        in_specs=[vmem],
        out_specs=(vmem, vmem),
        compiler_params=pltpu.CompilerParams(vmem_limit_bytes=40 * 2**20),
    )(received)


def sums_kernel(far, near, me_ref, weights_ref, points_ref, codes_ref, *refs):
    over = refs[:near]
    packed_hbm, tail, sem = refs[near + 1 :]
    owned = weights_ref.shape[2]
    listeners = over[0].shape[1]
    nwide, _, lanes = codes_ref.shape
    depth = packed_hbm.shape[1]
    step = min(256, owned)
    scale = TURN * TURN

    over_x = jnp.concatenate([over[n][2 * z : 2 * z + 1, :] for z in range(far) for n in range(near)], axis=1)
    over_y = jnp.concatenate([over[n][2 * z + 1 : 2 * z + 2, :] for z in range(far) for n in range(near)], axis=1)
    there = scale * (over_x * over_x + over_y * over_y + GROUND * GROUND)
    one, zero = jnp.ones_like(there), jnp.zeros_like(there)
    views = jnp.concatenate(
        thirds((-2.0 * scale) * over_x) + thirds((-2.0 * scale) * over_y) + thirds(there) + [one] * 3 + [zero] * 4,
        axis=0,
    ).astype(BF16)

    count = far * near * listeners
    width = min(256, count)
    for left in range(0, count, width):
        view = views[:, left : left + width]
        totals = [[None] * 4 for _ in range(HARM)]
        for start in range(0, owned, step):
            square = jnp.dot(points_ref[start : start + step, :], view, preferred_element_type=F32)
            inv = lax.rsqrt(square)
            turns = square * inv
            frac = turns - jnp.round(turns)
            half = horner(HALF_SINE, frac * frac) * frac
            versine = half * half
            cosine = 1.0 - versine
            twoc = cosine + cosine
            rest = jnp.maximum(2.0 - versine, 1e-30)
            c_prev, s_prev = inv, None
            c_now = inv * cosine
            s_now = (inv * half) * (rest * lax.rsqrt(rest))
            for h in range(HARM):
                ratio = inv * (TURN / (WAVENUMBER * (h + 1)))
                d, e = inv * c_now, inv * s_now
                part = weights_ref[h, :, start : start + step]
                for m, value in enumerate((c_now, s_now, ratio * d + e, d - ratio * e)):
                    product = jnp.dot(part, value.astype(BF16), preferred_element_type=F32)
                    totals[h][m] = product if start == 0 else totals[h][m] + product
                if h < HARM - 1:
                    c_next = twoc * c_now - c_prev
                    s_next = twoc * s_now - s_prev if h else twoc * s_now
                    c_prev, s_prev, c_now, s_now = c_now, s_now, c_next, s_next
        ox, oy = over_x[:, left : left + width], over_y[:, left : left + width]
        lines = []
        for h in range(HARM):
            factor = WAVENUMBER * (h + 1) * TURN
            cos_sum, sin_sum = totals[h][0], totals[h][1]

            def loads(m):
                t = totals[h][m]
                return [
                    ox * t[2 + c : 3 + c] + oy * t[4 + c : 5 + c] + (t[8 + c : 9 + c] + t[10 + c : 11 + c])
                    for c in (0, 1)
                ]

            (re_re, re_im), (im_re, im_im) = loads(2), loads(3)
            lines.append(factor * (sin_sum[0:1] - cos_sum[1:2] + TURN * (re_re - im_im)))
            lines.append(factor * (cos_sum[0:1] + sin_sum[1:2] + TURN * (re_im + im_re)))
        split = thirds(jnp.concatenate(lines, axis=0))
        for j in range(width // listeners):
            owner = me_ref[0] ^ (left // listeners + j)
            cells = [value[:, listeners * j : listeners * j + listeners] for value in split]
            cells.append(jnp.zeros((2 * HARM, lanes - 3 * listeners), F32))
            cells = jnp.concatenate(cells, axis=1)
            tail[owner] = jnp.concatenate([codes_ref[owner], cells], axis=0).astype(BF16)
    copy = pltpu.make_async_copy(tail, packed_hbm.at[:, depth - 16 : depth, :], sem)
    copy.start()
    copy.wait()


def pressure_sums(weights, points, codes, over, packed, far):
    near = len(over)
    listeners = over[0].shape[1]
    owned = weights.shape[2]
    nwide, depth, lanes = packed.shape
    vmem = pl.BlockSpec(memory_space=pltpu.VMEM)
    me = lax.axis_index("wide").reshape(1)

    def body(*refs):
        sums_kernel(far, near, *refs)

    return pl.pallas_call(
        body,
        out_shape=jax.ShapeDtypeStruct(packed.shape, BF16),
        in_specs=[pl.BlockSpec(memory_space=pltpu.SMEM)] + [vmem] * (3 + near) + [pl.BlockSpec(memory_space=pl.ANY)],
        out_specs=pl.BlockSpec(memory_space=pl.ANY),
        input_output_aliases={4 + near: 0},
        scratch_shapes=[pltpu.VMEM((nwide, 16, lanes), BF16), pltpu.SemaphoreType.DMA],
        compiler_params=pltpu.CompilerParams(vmem_limit_bytes=40 * 2**20),
        cost_estimate=pl.CostEstimate(
            flops=far * near * listeners * owned * 2000,
            bytes_accessed=owned * 70,
            transcendentals=far * near * listeners * owned,
        ),
    )(me, weights, points, codes, *over, packed)


def swap(x, nwide, bits):
    return lax.ppermute(x, "wide", [(i, i ^ bits) for i in range(nwide)])


def shards(flow, positions, normals, panel_ids, observers):
    owned = flow.shape[2]
    nwide = lax.axis_size("wide")
    listeners = observers.shape[1]
    far = 4
    near = nwide // far
    lines = jnp.concatenate([observers] + [swap(observers, nwide, near * z) for z in range(1, far)], axis=0)
    spectra, weights, points = sources(flow, normals, positions)
    lines, spectra = lax.optimization_barrier((lines, spectra))
    over = [lines] + [swap(lines, nwide, n) for n in range(1, near)]
    packed, codes = pack(spectra, panel_ids, nwide)
    packed = pressure_sums(weights, points, codes, over, packed, far)
    received = lax.all_to_all(packed, "wide", split_axis=0, concat_axis=0, tiled=True)
    panel_spectra, pressure = place(received, owned, listeners)
    return (panel_spectra, pressure.T)


def solution(mesh):
    placed = (
        P(None, None, ("case", "wide")),
        P(None, ("case", "wide")),
        P(None, ("case", "wide")),
        P(("case", "wide")),
        P(None, ("case", "wide")),
    )
    return jax.shard_map(
        shards,
        mesh=mesh,
        in_specs=placed,
        out_specs=(P(None, ("case", "wide")), P(("case", "wide"), None)),
        check_vma=False,
    )
```

```python
import math

import jax
import jax.numpy as jnp
import numpy as np
from jax import lax
from jax.experimental import pallas as pl
from jax.experimental.pallas import tpu as pltpu
from jax.sharding import PartitionSpec as P

NT = 16
HARM = 4
ROWS = 8 * HARM
WAVENUMBER = 2.0
GROUND = 3.0
LOW = 256
F32 = jnp.float32
BF16 = jnp.bfloat16
NT_DIMS = (((1,), (1,)), ((), ()))


def fit(function, degree):
    nodes = np.cos(np.pi * (np.arange(64) + 0.5) / 64) * 0.5
    squares = nodes * nodes
    powers = np.stack([squares**d for d in range(degree + 1)], axis=1)
    return [float(c) for c in np.linalg.lstsq(powers, function(nodes), rcond=None)[0]]


TURN = WAVENUMBER / (2.0 * math.pi)
HALF_SINE = fit(lambda f: math.sqrt(2.0) * np.sin(np.pi * f) / f, 4)


def horner(coefficients, x):
    value = coefficients[-1]
    for c in coefficients[-2::-1]:
        value = value * x + c
    return value


def thirds(x):
    first = x.astype(BF16).astype(F32)
    second = (x - first).astype(BF16).astype(F32)
    return [first, second, x - first - second]


def dft_split():
    samples = np.arange(NT)[:, None]
    harmonic = np.arange(1, HARM + 1)[None, :]
    angle = 2.0 * np.pi / NT * samples * harmonic
    table = np.stack([np.cos(angle), -np.sin(angle)], axis=2) * (2.0 / NT)
    table = table.reshape(NT, 2 * HARM).T
    block = np.kron(np.eye(4), table).astype(np.float32)
    order = [8 * a + 2 * h + c for h in range(HARM) for a in range(4) for c in range(2)]
    block = np.concatenate([block, block[order]], axis=0)
    high = block.astype(jnp.bfloat16)
    low = (block - high.astype(np.float32)).astype(jnp.bfloat16)
    return np.concatenate([high, high, low, low], axis=1)


def pack_shape(nwide, owned):
    capacity = 2 * owned // nwide
    lanes = min(capacity, 128)
    subs = capacity // lanes
    return capacity, lanes, subs, ROWS * subs + 16


def source_kernel(
    flow_hbm, normals_hbm, place_hbm, table_hbm, ids_hbm, over_hbm,
    spectra_ref, weights_ref, points_ref, ids_ref, mine_ref,
    flow_ref, normals_ref, place_ref, table_ref, sems,
):
    owned = flow_ref.shape[2]
    step = min(256, owned)
    pieces = 4
    wide = owned // pieces
    copies = [
        pltpu.make_async_copy(normals_hbm, normals_ref, sems.at[0]),
        pltpu.make_async_copy(place_hbm, place_ref, sems.at[1]),
        pltpu.make_async_copy(table_hbm, table_ref, sems.at[2]),
    ]
    passed = [
        pltpu.make_async_copy(ids_hbm, ids_ref, sems.at[3]),
        pltpu.make_async_copy(over_hbm, mine_ref, sems.at[4]),
    ]
    flows = [
        pltpu.make_async_copy(
            flow_hbm.at[:, :, wide * p : wide * p + wide], flow_ref.at[:, :, wide * p : wide * p + wide], sems.at[5 + p]
        )
        for p in range(pieces)
    ]
    for copy in copies + flows + passed:
        copy.start()
    for copy in copies:
        copy.wait()
    table = table_ref[...]
    scale = TURN * TURN
    for start in range(0, owned, step):
        if start % wide == 0:
            flows[start // wide].wait()
        cols = slice(start, start + step)
        normal = normals_ref[:, cols].astype(F32)
        n0, n1, n2 = normal[0:1], normal[1:2], normal[2:3]
        density = 1.0 + 0.2 * flow_ref[0, :, cols].astype(F32)
        v0 = 0.5 * flow_ref[1, :, cols].astype(F32)
        v1 = 0.5 * flow_ref[2, :, cols].astype(F32)
        v2 = 0.5 * flow_ref[3, :, cols].astype(F32)
        fluct = flow_ref[4, :, cols].astype(F32)
        across = v0 * n0 + v1 * n1 + v2 * n2
        source = density * across
        parts = jnp.concatenate(
            [source, fluct * n0 + v0 * source, fluct * n1 + v1 * source, fluct * n2 + v2 * source], axis=0
        )
        top = parts.astype(BF16)
        rest = (parts - top.astype(F32)).astype(BF16)
        both = jnp.concatenate([top, rest, top, rest], axis=0)
        spectra = jnp.dot(table, both, preferred_element_type=F32).astype(BF16)
        spectra_ref[:, cols] = spectra[:ROWS]
        by_harmonic = spectra[ROWS:].astype(F32)
        place = place_ref[:, cols].astype(F32)
        px, py, pz = place[0:1], place[1:2], place[2:3]
        down = pz + GROUND
        none = jnp.zeros_like(px)
        factors = jnp.concatenate([none, none, px, px, py, py, down, down], axis=0)
        for h in range(HARM):
            group = by_harmonic[8 * h : 8 * h + 8]
            shares = group * factors
            along = -(shares[2:4] + shares[4:6] + shares[6:8])
            along_high = along.astype(BF16).astype(F32)
            weights_ref[h, :, cols] = jnp.concatenate(
                [group, along_high, along - along_high, jnp.zeros((4, step), F32)], axis=0
            ).astype(BF16)
        here = scale * (px * px + py * py + pz * pz + (2.0 * GROUND) * pz)
        one = jnp.ones_like(here)
        points = jnp.concatenate([px] * 3 + [py] * 3 + [one] * 3 + thirds(here) + [none] * 4, axis=0)
        points_ref[cols, :] = points.T.astype(BF16)
    for copy in passed:
        copy.wait()


def sources(flow, normals, positions, ids, observers):
    owned = flow.shape[2]
    vmem = pl.BlockSpec(memory_space=pltpu.VMEM)
    anywhere = pl.BlockSpec(memory_space=pl.ANY)
    table = jnp.asarray(dft_split())
    arrays = (flow, normals, positions, table, ids.reshape(1, owned), observers)
    return pl.pallas_call(
        source_kernel,
        out_shape=(
            jax.ShapeDtypeStruct((ROWS, owned), BF16),
            jax.ShapeDtypeStruct((HARM, 16, owned), BF16),
            jax.ShapeDtypeStruct((owned, 16), BF16),
            jax.ShapeDtypeStruct((1, owned), jnp.int32),
            jax.ShapeDtypeStruct(observers.shape, F32),
        ),
        in_specs=[anywhere] * 6,
        out_specs=(vmem,) * 5,
        scratch_shapes=[
            pltpu.VMEM(flow.shape, BF16),
            pltpu.VMEM(normals.shape, BF16),
            pltpu.VMEM(positions.shape, BF16),
            pltpu.VMEM(table.shape, BF16),
            pltpu.SemaphoreType.DMA((9,)),
        ],
        compiler_params=pltpu.CompilerParams(vmem_limit_bytes=32 * 2**20),
    )(*(pltpu.with_memory_space_constraint(x, pltpu.HBM) for x in arrays))


def pack_kernel(nwide, spectra_ref, ids_ref, packed_ref, codes_ref, left, right):
    owned = spectra_ref.shape[1]
    capacity, lanes, subs, _ = pack_shape(nwide, owned)
    step = min(256, owned)
    upper = (
        lax.broadcasted_iota(jnp.int32, (step, step), 0)
        < lax.broadcasted_iota(jnp.int32, (step, step), 1)
    ).astype(F32).astype(BF16)
    ids = ids_ref[...]
    owner = ids // owned
    local = ids - owner * owned
    high = local // LOW
    code_high = (high + 1).astype(F32)
    code_low = (local - high * LOW).astype(F32)
    carry = jnp.zeros((nwide, 1), F32)
    which = lax.broadcasted_iota(jnp.int32, (nwide, step), 0)
    slots = lax.broadcasted_iota(jnp.int32, (capacity, step), 0).astype(F32)
    codes_row = lax.broadcasted_iota(jnp.int32, (8, step), 0)
    for start in range(0, owned, step):
        cols = slice(start, start + step)
        own = which == owner[:, cols]
        ownf = own.astype(F32)
        before = jnp.dot(ownf.astype(BF16), upper, preferred_element_type=F32) + carry
        rank = jnp.sum(before * ownf, axis=0, keepdims=True)
        carry = before[:, step - 1 : step] + ownf[:, step - 1 : step]
        right[:, cols] = (slots == rank).astype(F32).astype(BF16)
        codes = jnp.where(codes_row == 0, code_high[:, cols], jnp.where(codes_row == 1, code_low[:, cols], 0.0))
        codes = jnp.concatenate([codes, jnp.zeros_like(codes)], axis=0).astype(BF16)
        values = jnp.concatenate([spectra_ref[:, cols], codes], axis=0)
        for o in range(nwide):
            left[48 * o : 48 * o + 48, cols] = jnp.where(owner[:, cols] == o, values, jnp.zeros_like(values))
    packed = lax.dot_general(left[...], right[...], NT_DIMS, preferred_element_type=F32)
    for o in range(nwide):
        block = packed[48 * o : 48 * o + 48]
        for s in range(subs):
            packed_ref[o, ROWS * s : ROWS * s + ROWS, :] = block[:ROWS, lanes * s : lanes * s + lanes].astype(BF16)
        codes = [block[ROWS : ROWS + 2, lanes * s : lanes * s + lanes] for s in range(subs)]
        codes_ref[o] = jnp.concatenate(codes + [jnp.zeros((8 - 2 * subs, lanes), F32)], axis=0)


def pack(spectra, ids, nwide):
    owned = spectra.shape[1]
    capacity, lanes, subs, depth = pack_shape(nwide, owned)
    vmem = pl.BlockSpec(memory_space=pltpu.VMEM)

    def body(*refs):
        pack_kernel(nwide, *refs)

    return pl.pallas_call(
        body,
        out_shape=(
            jax.ShapeDtypeStruct((nwide, depth, lanes), BF16),
            jax.ShapeDtypeStruct((nwide, 8, lanes), F32),
        ),
        in_specs=[vmem] * 2,
        out_specs=(vmem, vmem),
        scratch_shapes=[
            pltpu.VMEM((48 * nwide, owned), BF16),
            pltpu.VMEM((capacity, owned), BF16),
        ],
        compiler_params=pltpu.CompilerParams(vmem_limit_bytes=40 * 2**20),
    )(spectra, ids)


def place_kernel(scale, received_ref, spectra_ref, pressure_ref):
    nwide, depth, lanes = received_ref.shape
    owned = spectra_ref.shape[1]
    listeners = pressure_ref.shape[1]
    subs = (depth - 16) // ROWS
    heights = owned // LOW
    group = max(1, 256 // (lanes * subs))
    width = lanes * subs * group
    lows = lax.broadcasted_iota(jnp.int32, (LOW, width), 0).astype(F32)
    total = jnp.zeros((heights * ROWS, LOW), F32)
    sums = jnp.zeros((2 * HARM, lanes), F32)
    for first in range(0, nwide, group):
        blocks, high, low = [], [], []
        for o in range(first, first + group):
            codes = received_ref[o, ROWS * subs : ROWS * subs + 16, :].astype(F32)
            sums = sums + codes[8:16]
            for s in range(subs):
                blocks.append(received_ref[o, ROWS * s : ROWS * s + ROWS, :])
                high.append(codes[2 * s : 2 * s + 1])
                low.append(codes[2 * s + 1 : 2 * s + 2])
        values = jnp.concatenate(blocks, axis=1)
        high = jnp.concatenate(high, axis=1)
        low = jnp.concatenate(low, axis=1)
        spread = (lows == low).astype(F32).astype(BF16)
        picked = jnp.concatenate(
            [jnp.where(high == h + 1.0, values, jnp.zeros_like(values)) for h in range(heights)], axis=0
        )
        total = total + lax.dot_general(picked, spread, NT_DIMS, preferred_element_type=F32)
    for h in range(heights):
        spectra_ref[:, LOW * h : LOW * h + LOW] = total[ROWS * h : ROWS * h + ROWS].astype(BF16)
    third = [sums[:, listeners * p : listeners * p + listeners] for p in range(3)]
    pressure_ref[...] = scale * ((third[2] + third[1]) + third[0])


def place(received, owned, listeners):
    nwide = received.shape[0]
    vmem = pl.BlockSpec(memory_space=pltpu.VMEM)
    scale = 2.0 / math.sqrt(owned * nwide)

    def body(*refs):
        place_kernel(scale, *refs)

    return pl.pallas_call(
        body,
        out_shape=(
            jax.ShapeDtypeStruct((ROWS, owned), BF16),
            jax.ShapeDtypeStruct((2 * HARM, listeners), F32),
        ),
        in_specs=[vmem],
        out_specs=(vmem, vmem),
        compiler_params=pltpu.CompilerParams(vmem_limit_bytes=40 * 2**20),
    )(received)


SUB = 64
KINDS = 6


def pair_sums(lines, weights_ref, points_ref):
    owned = weights_ref.shape[2]
    count = lines.shape[0] // 2
    listeners = lines.shape[1]
    step = min(256, owned)
    scale = TURN * TURN
    over_x = jnp.concatenate([lines[2 * j : 2 * j + 1] for j in range(count)], axis=1)
    over_y = jnp.concatenate([lines[2 * j + 1 : 2 * j + 2] for j in range(count)], axis=1)
    there = scale * (over_x * over_x + over_y * over_y + GROUND * GROUND)
    one, zero = jnp.ones_like(there), jnp.zeros_like(there)
    views = jnp.concatenate(
        thirds((-2.0 * scale) * over_x) + thirds((-2.0 * scale) * over_y) + thirds(there) + [one] * 3 + [zero] * 4,
        axis=0,
    ).astype(BF16)
    width = min(256, count * listeners)
    made = []
    for left in range(0, count * listeners, width):
        view = views[:, left : left + width]
        totals = [[None] * KINDS for _ in range(HARM)]
        pending = []

        def drain(number):
            for _ in range(min(number, len(pending))):
                h, m, begin, pieces = pending.pop(0)
                whole = pieces[0] if len(pieces) == 1 else jnp.concatenate(pieces, axis=0)
                part = weights_ref[h, :, begin : begin + step]
                product = jnp.dot(part, whole, preferred_element_type=F32)
                totals[h][m] = product if totals[h][m] is None else totals[h][m] + product

        for start in range(0, owned, step):
            mats = [[[] for _ in range(KINDS)] for _ in range(HARM)]
            for row in range(start, start + step, SUB):
                square = jnp.dot(points_ref[row : row + SUB, :], view, preferred_element_type=F32)
                inv = lax.rsqrt(square)
                turns = square * inv
                frac = turns - jnp.round(turns)
                half = horner(HALF_SINE, frac * frac) * frac
                versine = half * half
                cosine = 1.0 - versine
                twoc = cosine + cosine
                rest = jnp.maximum(2.0 - versine, 1e-30)
                inv2 = (inv * inv).astype(BF16)
                c_prev, s_prev = inv, None
                c_now = inv * cosine
                s_now = (inv * half) * (rest * lax.rsqrt(rest))
                for h in range(HARM):
                    c_bf, s_bf = c_now.astype(BF16), s_now.astype(BF16)
                    d, e = (inv * c_now).astype(BF16), (inv * s_now).astype(BF16)
                    for m, value in enumerate((c_bf, s_bf, d, e, inv2 * c_bf, inv2 * s_bf)):
                        mats[h][m].append(value)
                    if h < HARM - 1:
                        c_next = twoc * c_now - c_prev
                        s_next = twoc * s_now - s_prev if h else twoc * s_now
                        c_prev, s_prev, c_now, s_now = c_now, s_now, c_next, s_next
                drain(HARM * KINDS * SUB // step)
            drain(HARM * KINDS)
            pending += [(h, m, start, mats[h][m]) for h in range(HARM) for m in range(KINDS)]
        drain(HARM * KINDS)
        ox, oy = over_x[:, left : left + width], over_y[:, left : left + width]
        rows = []
        for h in range(HARM):
            wavenum = WAVENUMBER * (h + 1)
            cos_sum, sin_sum = totals[h][0], totals[h][1]

            def loads(m):
                t = totals[h][m]
                return [
                    ox * t[2 + c : 3 + c] + oy * t[4 + c : 5 + c] + (t[8 + c : 9 + c] + t[10 + c : 11 + c])
                    for c in (0, 1)
                ]

            (dr, di), (er, ei), (ur, ui), (vr, vi) = loads(2), loads(3), loads(4), loads(5)
            real = wavenum * (er - di) + TURN * (ur + vi)
            imag = wavenum * (ei + dr) + TURN * (ui - vr)
            rows.append(TURN * (wavenum * (sin_sum[0:1] - cos_sum[1:2]) + TURN * real))
            rows.append(TURN * (wavenum * (cos_sum[0:1] + sin_sum[1:2]) + TURN * imag))
        made.append(jnp.concatenate(rows, axis=0))
    return made


def cells_of(lines, weights_ref, points_ref, lanes):
    listeners = lines.shape[1]
    cells = []
    for value in pair_sums(lines, weights_ref, points_ref):
        split = thirds(value)
        for j in range(value.shape[1] // listeners):
            cell = [third[:, listeners * j : listeners * j + listeners] for third in split]
            cell.append(jnp.zeros((2 * HARM, lanes - 3 * listeners), F32))
            cells.append(jnp.concatenate(cell, axis=1))
    return cells


def first_kernel(lines_ref, weights_ref, points_ref, cells_ref):
    for j, cell in enumerate(cells_of(lines_ref[...], weights_ref, points_ref, cells_ref.shape[2])):
        cells_ref[j] = cell


def second_kernel(
    steps, me_ref, lines_ref, weights_ref, points_ref, cells_ref, codes_ref, packed_in, packed_hbm, tail, sem
):
    lanes = codes_ref.shape[2]
    depth = packed_hbm.shape[1]
    early = cells_ref.shape[0]
    cells = [cells_ref[j] for j in range(early)]
    cells += cells_of(lines_ref[...], weights_ref, points_ref, lanes)
    for j, cell in enumerate(cells):
        owner = me_ref[0] ^ steps[j]
        tail[owner] = jnp.concatenate([codes_ref[owner], cell], axis=0).astype(BF16)
    copy = pltpu.make_async_copy(tail, packed_hbm.at[:, depth - 16 : depth, :], sem)
    copy.start()
    copy.wait()


def first_sums(lines, weights, points, lanes):
    owned = weights.shape[2]
    devices = lines.shape[0] // 2
    pairs = devices * lines.shape[1] * owned
    vmem = pl.BlockSpec(memory_space=pltpu.VMEM)
    return pl.pallas_call(
        first_kernel,
        out_shape=jax.ShapeDtypeStruct((devices, 2 * HARM, lanes), F32),
        in_specs=[vmem] * 3,
        out_specs=vmem,
        compiler_params=pltpu.CompilerParams(vmem_limit_bytes=40 * 2**20),
        cost_estimate=pl.CostEstimate(flops=pairs * 2000, bytes_accessed=owned * 70, transcendentals=pairs),
    )(lines, weights, points)


def second_sums(lines, weights, points, cells, codes, packed, steps):
    owned = weights.shape[2]
    nwide, depth, lanes = packed.shape
    pairs = lines.shape[0] // 2 * lines.shape[1] * owned
    vmem = pl.BlockSpec(memory_space=pltpu.VMEM)
    anywhere = pl.BlockSpec(memory_space=pl.ANY)
    me = lax.axis_index("wide").reshape(1)

    def body(*refs):
        second_kernel(steps, *refs)

    return pl.pallas_call(
        body,
        out_shape=jax.ShapeDtypeStruct(packed.shape, BF16),
        in_specs=[pl.BlockSpec(memory_space=pltpu.SMEM)] + [vmem] * 5 + [anywhere],
        out_specs=anywhere,
        input_output_aliases={6: 0},
        scratch_shapes=[pltpu.VMEM((nwide, 16, lanes), BF16), pltpu.SemaphoreType.DMA],
        compiler_params=pltpu.CompilerParams(vmem_limit_bytes=40 * 2**20),
        cost_estimate=pl.CostEstimate(flops=pairs * 2000, bytes_accessed=owned * 70, transcendentals=pairs),
    )(me, lines, weights, points, cells, codes, packed)


def swap(x, nwide, bit):
    return lax.ppermute(x, "wide", [(i, i ^ bit) for i in range(nwide)])


def shards(flow, positions, normals, panel_ids, observers):
    owned = flow.shape[2]
    nwide = lax.axis_size("wide")
    listeners = observers.shape[1]
    near = nwide // 4
    others = [swap(observers, nwide, n) for n in range(1, near)]
    spectra, weights, points, ids, mine = sources(flow, normals, positions, panel_ids, observers)
    others, spectra = lax.optimization_barrier((others, spectra))
    lines = jnp.concatenate([mine] + others, axis=0)
    other = swap(lines, nwide, near)
    packed, codes = pack(spectra, ids, nwide)
    other, packed = lax.optimization_barrier((other, packed))
    lines = jnp.concatenate([lines, other], axis=0)
    other = swap(lines, nwide, 2 * near)
    cells = first_sums(lines, weights, points, packed.shape[2])
    other, cells = lax.optimization_barrier((other, cells))
    steps = [n ^ z for z in range(0, 4 * near, near) for n in range(near)]
    packed = second_sums(other, weights, points, cells, codes, packed, steps)
    received = lax.all_to_all(packed, "wide", split_axis=0, concat_axis=0, tiled=True)
    panel_spectra, pressure = place(received, owned, listeners)
    return (panel_spectra, pressure.T)


def solution(mesh):
    placed = (
        P(None, None, ("case", "wide")),
        P(None, ("case", "wide")),
        P(None, ("case", "wide")),
        P(("case", "wide")),
        P(None, ("case", "wide")),
    )
    return jax.shard_map(
        shards,
        mesh=mesh,
        in_specs=placed,
        out_specs=(P(None, ("case", "wide")), P(("case", "wide"), None)),
        check_vma=False,
    )
```

```python
import math

import jax
import jax.numpy as jnp
import numpy as np
from jax import lax
from jax.experimental import pallas as pl
from jax.experimental.pallas import tpu as pltpu
from jax.sharding import PartitionSpec as P

NT = 16
HARM = 4
ROWS = 8 * HARM
WAVENUMBER = 2.0
GROUND = 3.0
LOW = 256
F32 = jnp.float32
BF16 = jnp.bfloat16
NT_DIMS = (((1,), (1,)), ((), ()))


def fit(function, degree):
    nodes = np.cos(np.pi * (np.arange(64) + 0.5) / 64) * 0.5
    squares = nodes * nodes
    powers = np.stack([squares**d for d in range(degree + 1)], axis=1)
    return [float(c) for c in np.linalg.lstsq(powers, function(nodes), rcond=None)[0]]


TURN = WAVENUMBER / (2.0 * math.pi)
HALF_SINE = fit(lambda f: math.sqrt(2.0) * (1.0 - 1e-6) * np.sin(np.pi * f) / f, 4)


def horner(coefficients, x):
    value = coefficients[-1]
    for c in coefficients[-2::-1]:
        value = value * x + c
    return value


def thirds(x):
    first = x.astype(BF16).astype(F32)
    second = (x - first).astype(BF16).astype(F32)
    return [first, second, x - first - second]


def dft_split():
    samples = np.arange(NT)[:, None]
    harmonic = np.arange(1, HARM + 1)[None, :]
    angle = 2.0 * np.pi / NT * samples * harmonic
    table = np.stack([np.cos(angle), -np.sin(angle)], axis=2) * (2.0 / NT)
    table = table.reshape(NT, 2 * HARM).T
    block = np.kron(np.eye(4), table).astype(np.float32)
    order = [8 * a + 2 * h + c for h in range(HARM) for a in range(4) for c in range(2)]
    block = np.concatenate([block, block[order]], axis=0)
    high = block.astype(jnp.bfloat16)
    low = (block - high.astype(np.float32)).astype(jnp.bfloat16)
    return np.concatenate([high, high, low, low], axis=1)


def pack_shape(nwide, owned):
    capacity = 2 * owned // nwide
    lanes = min(capacity, 128)
    subs = capacity // lanes
    return capacity, lanes, subs, ROWS * subs + 8


def source_kernel(
    flow_hbm, normals_hbm, place_hbm, table_hbm, ids_hbm, over_hbm,
    spectra_ref, weights_ref, points_ref, ids_ref, mine_ref,
    flow_ref, normals_ref, place_ref, table_ref, sems,
):
    owned = flow_ref.shape[2]
    step = min(256, owned)
    pieces = 4
    wide = owned // pieces
    copies = [
        pltpu.make_async_copy(normals_hbm, normals_ref, sems.at[0]),
        pltpu.make_async_copy(place_hbm, place_ref, sems.at[1]),
        pltpu.make_async_copy(table_hbm, table_ref, sems.at[2]),
    ]
    passed = [
        pltpu.make_async_copy(ids_hbm, ids_ref, sems.at[3]),
        pltpu.make_async_copy(over_hbm, mine_ref, sems.at[4]),
    ]
    flows = [
        pltpu.make_async_copy(
            flow_hbm.at[:, :, wide * p : wide * p + wide], flow_ref.at[:, :, wide * p : wide * p + wide], sems.at[5 + p]
        )
        for p in range(pieces)
    ]
    for copy in copies + flows + passed:
        copy.start()
    for copy in copies:
        copy.wait()
    table = table_ref[...]
    scale = TURN * TURN
    for start in range(0, owned, step):
        if start % wide == 0:
            flows[start // wide].wait()
        cols = slice(start, start + step)
        normal = normals_ref[:, cols].astype(F32)
        n0, n1, n2 = normal[0:1], normal[1:2], normal[2:3]
        density = 1.0 + 0.2 * flow_ref[0, :, cols].astype(F32)
        v0 = 0.5 * flow_ref[1, :, cols].astype(F32)
        v1 = 0.5 * flow_ref[2, :, cols].astype(F32)
        v2 = 0.5 * flow_ref[3, :, cols].astype(F32)
        fluct = flow_ref[4, :, cols].astype(F32)
        across = v0 * n0 + v1 * n1 + v2 * n2
        source = density * across
        parts = jnp.concatenate(
            [source, fluct * n0 + v0 * source, fluct * n1 + v1 * source, fluct * n2 + v2 * source], axis=0
        )
        top = parts.astype(BF16)
        rest = (parts - top.astype(F32)).astype(BF16)
        both = jnp.concatenate([top, rest, top, rest], axis=0)
        spectra = jnp.dot(table, both, preferred_element_type=F32).astype(BF16)
        spectra_ref[:, cols] = spectra[:ROWS]
        by_harmonic = spectra[ROWS:].astype(F32)
        place = place_ref[:, cols].astype(F32)
        px, py, pz = place[0:1], place[1:2], place[2:3]
        down = pz + GROUND
        none = jnp.zeros_like(px)
        factors = jnp.concatenate([none, none, px, px, py, py, down, down], axis=0)
        for h in range(HARM):
            group = by_harmonic[8 * h : 8 * h + 8]
            shares = group * factors
            along = -(shares[2:4] + shares[4:6] + shares[6:8])
            along_high = along.astype(BF16).astype(F32)
            weights_ref[h, :, cols] = jnp.concatenate(
                [group, along_high, along - along_high, jnp.zeros((4, step), F32)], axis=0
            ).astype(BF16)
        here = scale * (px * px + py * py + pz * pz + (2.0 * GROUND) * pz)
        one = jnp.ones_like(here)
        points = jnp.concatenate([px] * 3 + [py] * 3 + [one] * 3 + thirds(here) + [none] * 4, axis=0)
        points_ref[cols, :] = points.T.astype(BF16)
    for copy in passed:
        copy.wait()


def sources(flow, normals, positions, ids, observers):
    owned = flow.shape[2]
    vmem = pl.BlockSpec(memory_space=pltpu.VMEM)
    anywhere = pl.BlockSpec(memory_space=pl.ANY)
    table = jnp.asarray(dft_split())
    arrays = (flow, normals, positions, table, ids.reshape(1, owned), observers)
    return pl.pallas_call(
        source_kernel,
        out_shape=(
            jax.ShapeDtypeStruct((ROWS, owned), BF16),
            jax.ShapeDtypeStruct((HARM, 16, owned), BF16),
            jax.ShapeDtypeStruct((owned, 16), BF16),
            jax.ShapeDtypeStruct((1, owned), jnp.int32),
            jax.ShapeDtypeStruct(observers.shape, F32),
        ),
        in_specs=[anywhere] * 6,
        out_specs=(vmem,) * 5,
        scratch_shapes=[
            pltpu.VMEM(flow.shape, BF16),
            pltpu.VMEM(normals.shape, BF16),
            pltpu.VMEM(positions.shape, BF16),
            pltpu.VMEM(table.shape, BF16),
            pltpu.SemaphoreType.DMA((9,)),
        ],
        compiler_params=pltpu.CompilerParams(vmem_limit_bytes=32 * 2**20),
    )(*(pltpu.with_memory_space_constraint(x, pltpu.HBM) for x in arrays))


def pack_kernel(nwide, spectra_ref, ids_ref, packed_ref, codes_ref, left, right):
    owned = spectra_ref.shape[1]
    capacity, lanes, subs, _ = pack_shape(nwide, owned)
    step = min(256, owned)
    upper = (
        lax.broadcasted_iota(jnp.int32, (step, step), 0)
        < lax.broadcasted_iota(jnp.int32, (step, step), 1)
    ).astype(F32).astype(BF16)
    ids = ids_ref[...]
    owner = ids // owned
    local = ids - owner * owned
    high = local // LOW
    code_high = (high + 1).astype(F32)
    code_low = (local - high * LOW).astype(F32)
    carry = jnp.zeros((nwide, 1), F32)
    which = lax.broadcasted_iota(jnp.int32, (nwide, step), 0)
    slots = lax.broadcasted_iota(jnp.int32, (capacity, step), 0).astype(F32)
    codes_row = lax.broadcasted_iota(jnp.int32, (8, step), 0)
    for start in range(0, owned, step):
        cols = slice(start, start + step)
        own = which == owner[:, cols]
        ownf = own.astype(F32)
        before = jnp.dot(ownf.astype(BF16), upper, preferred_element_type=F32) + carry
        rank = jnp.sum(before * ownf, axis=0, keepdims=True)
        carry = before[:, step - 1 : step] + ownf[:, step - 1 : step]
        right[:, cols] = (slots == rank).astype(F32).astype(BF16)
        codes = jnp.where(codes_row == 0, code_high[:, cols], jnp.where(codes_row == 1, code_low[:, cols], 0.0))
        codes = jnp.concatenate([codes, jnp.zeros_like(codes)], axis=0).astype(BF16)
        values = jnp.concatenate([spectra_ref[:, cols], codes], axis=0)
        for o in range(nwide):
            left[48 * o : 48 * o + 48, cols] = jnp.where(owner[:, cols] == o, values, jnp.zeros_like(values))
    packed = lax.dot_general(left[...], right[...], NT_DIMS, preferred_element_type=F32)
    lane = lax.broadcasted_iota(jnp.int32, (8, lanes), 1)
    for o in range(nwide):
        block = packed[48 * o : 48 * o + 48]
        for s in range(subs):
            packed_ref[o, ROWS * s : ROWS * s + ROWS, :] = block[:ROWS, lanes * s : lanes * s + lanes].astype(BF16)
        codes = []
        for s in range(subs):
            upper_half = block[ROWS : ROWS + 8, lanes * s : lanes * s + lanes]
            lower_half = jnp.concatenate([upper_half[:, lanes // 2 :], upper_half[:, : lanes // 2]], axis=1)
            codes += [lower_half[:2], upper_half[:2]]
        codes = jnp.concatenate(codes + [jnp.zeros((8 - 4 * subs, lanes), F32)] * (subs == 1), axis=0)
        codes_ref[o] = jnp.where(lane < lanes // 2, 0.0, codes)


def pack(spectra, ids, nwide):
    owned = spectra.shape[1]
    capacity, lanes, subs, _ = pack_shape(nwide, owned)
    vmem = pl.BlockSpec(memory_space=pltpu.VMEM)

    def body(*refs):
        pack_kernel(nwide, *refs)

    return pl.pallas_call(
        body,
        out_shape=(
            jax.ShapeDtypeStruct((nwide, ROWS * subs, lanes), BF16),
            jax.ShapeDtypeStruct((nwide, 8, lanes), F32),
        ),
        in_specs=[vmem] * 2,
        out_specs=(vmem, vmem),
        scratch_shapes=[
            pltpu.VMEM((48 * nwide, owned), BF16),
            pltpu.VMEM((capacity, owned), BF16),
        ],
        compiler_params=pltpu.CompilerParams(vmem_limit_bytes=40 * 2**20),
    )(spectra, ids)


def place_kernel(scale, received_ref, spectra_ref, pressure_ref):
    nwide, depth, lanes = received_ref.shape
    owned = spectra_ref.shape[1]
    listeners = pressure_ref.shape[1]
    subs = (depth - 8) // ROWS
    heights = owned // LOW
    group = max(1, 256 // (lanes * subs))
    width = lanes * subs * group
    lows = lax.broadcasted_iota(jnp.int32, (LOW, width), 0).astype(F32)
    total = jnp.zeros((heights * ROWS, LOW), F32)
    sums = jnp.zeros((2 * HARM, lanes), F32)
    lower = lax.broadcasted_iota(jnp.int32, (1, lanes), 1) < lanes // 2
    for first in range(0, nwide, group):
        blocks, high, low = [], [], []
        for o in range(first, first + group):
            codes = received_ref[o, ROWS * subs : ROWS * subs + 8, :].astype(F32)
            sums = sums + codes
            turned = jnp.concatenate([codes[:, lanes // 2 :], codes[:, : lanes // 2]], axis=1)
            for s in range(subs):
                blocks.append(received_ref[o, ROWS * s : ROWS * s + ROWS, :])
                high.append(jnp.where(lower, turned[4 * s : 4 * s + 1], codes[4 * s + 2 : 4 * s + 3]))
                low.append(jnp.where(lower, turned[4 * s + 1 : 4 * s + 2], codes[4 * s + 3 : 4 * s + 4]))
        values = jnp.concatenate(blocks, axis=1)
        high = jnp.concatenate(high, axis=1)
        low = jnp.concatenate(low, axis=1)
        spread = (lows == low).astype(F32).astype(BF16)
        picked = jnp.concatenate(
            [jnp.where(high == h + 1.0, values, jnp.zeros_like(values)) for h in range(heights)], axis=0
        )
        total = total + lax.dot_general(picked, spread, NT_DIMS, preferred_element_type=F32)
    for h in range(heights):
        spectra_ref[:, LOW * h : LOW * h + LOW] = total[ROWS * h : ROWS * h + ROWS].astype(BF16)
    pressure_ref[...] = scale * (sums[:, listeners : 2 * listeners] + sums[:, :listeners])


def place(received, owned, listeners):
    nwide = received.shape[0]
    vmem = pl.BlockSpec(memory_space=pltpu.VMEM)
    scale = 2.0 / math.sqrt(owned * nwide)

    def body(*refs):
        place_kernel(scale, *refs)

    return pl.pallas_call(
        body,
        out_shape=(
            jax.ShapeDtypeStruct((ROWS, owned), BF16),
            jax.ShapeDtypeStruct((2 * HARM, listeners), F32),
        ),
        in_specs=[vmem],
        out_specs=(vmem, vmem),
        compiler_params=pltpu.CompilerParams(vmem_limit_bytes=40 * 2**20),
    )(received)


SUB = 64
KINDS = 6


def pair_sums(lines, weights_ref, points_ref):
    owned = weights_ref.shape[2]
    count = lines.shape[0] // 2
    listeners = lines.shape[1]
    step = min(256, owned)
    scale = TURN * TURN
    over_x = jnp.concatenate([lines[2 * j : 2 * j + 1] for j in range(count)], axis=1)
    over_y = jnp.concatenate([lines[2 * j + 1 : 2 * j + 2] for j in range(count)], axis=1)
    there = scale * (over_x * over_x + over_y * over_y + GROUND * GROUND)
    one, zero = jnp.ones_like(there), jnp.zeros_like(there)
    views = jnp.concatenate(
        thirds((-2.0 * scale) * over_x) + thirds((-2.0 * scale) * over_y) + thirds(there) + [one] * 3 + [zero] * 4,
        axis=0,
    ).astype(BF16)
    width = min(256, count * listeners)
    made = []
    for left in range(0, count * listeners, width):
        view = views[:, left : left + width]
        totals = [[None] * KINDS for _ in range(HARM)]
        pending = []

        def drain(number):
            for _ in range(min(number, len(pending))):
                h, m, begin, pieces = pending.pop(0)
                whole = pieces[0] if len(pieces) == 1 else jnp.concatenate(pieces, axis=0)
                part = weights_ref[h, :, begin : begin + step]
                product = jnp.dot(part, whole, preferred_element_type=F32)
                totals[h][m] = product if totals[h][m] is None else totals[h][m] + product

        for start in range(0, owned, step):
            mats = [[[] for _ in range(KINDS)] for _ in range(HARM)]
            for row in range(start, start + step, SUB):
                square = jnp.dot(points_ref[row : row + SUB, :], view, preferred_element_type=F32)
                inv = lax.rsqrt(square)
                turns = square * inv
                frac = turns - jnp.round(turns)
                half = horner(HALF_SINE, frac * frac) * frac
                versine = half * half
                cosine = 1.0 - versine
                twoc = cosine + cosine
                rest = 2.0 - versine
                inv_bf = inv.astype(BF16)
                c_prev, s_prev = inv, None
                c_now = inv * cosine
                s_now = (inv * half) * (rest * lax.rsqrt(rest))
                for h in range(HARM):
                    c_bf, s_bf = c_now.astype(BF16), s_now.astype(BF16)
                    d, e = (inv * c_now).astype(BF16), (inv * s_now).astype(BF16)
                    for m, value in enumerate((c_bf, s_bf, d, e, inv_bf * d, inv_bf * e)):
                        mats[h][m].append(value)
                    if h < HARM - 1:
                        c_next = twoc * c_now - c_prev
                        s_next = twoc * s_now - s_prev if h else twoc * s_now
                        c_prev, s_prev, c_now, s_now = c_now, s_now, c_next, s_next
                drain(HARM * KINDS * SUB // step)
            drain(HARM * KINDS)
            pending += [(h, m, start, mats[h][m]) for h in range(HARM) for m in range(KINDS)]
        drain(HARM * KINDS)
        ox, oy = over_x[:, left : left + width], over_y[:, left : left + width]
        rows = []
        for h in range(HARM):
            wavenum = WAVENUMBER * (h + 1)
            cos_sum, sin_sum = totals[h][0], totals[h][1]

            def loads(m):
                t = totals[h][m]
                return [
                    ox * t[2 + c : 3 + c] + oy * t[4 + c : 5 + c] + (t[8 + c : 9 + c] + t[10 + c : 11 + c])
                    for c in (0, 1)
                ]

            (dr, di), (er, ei), (ur, ui), (vr, vi) = loads(2), loads(3), loads(4), loads(5)
            real = wavenum * (er - di) + TURN * (ur + vi)
            imag = wavenum * (ei + dr) + TURN * (ui - vr)
            rows.append(TURN * (wavenum * (sin_sum[0:1] - cos_sum[1:2]) + TURN * real))
            rows.append(TURN * (wavenum * (cos_sum[0:1] + sin_sum[1:2]) + TURN * imag))
        made.append(jnp.concatenate(rows, axis=0))
    return made


def cells_of(lines, weights_ref, points_ref, lanes):
    listeners = lines.shape[1]
    cells = []
    for value in pair_sums(lines, weights_ref, points_ref):
        top = value.astype(BF16).astype(F32)
        split = [top, value - top]
        for j in range(value.shape[1] // listeners):
            cell = [half[:, listeners * j : listeners * j + listeners] for half in split]
            cell.append(jnp.zeros((2 * HARM, lanes - 2 * listeners), F32))
            cells.append(jnp.concatenate(cell, axis=1))
    return cells


def first_kernel(lines_ref, weights_ref, points_ref, cells_ref):
    for j, cell in enumerate(cells_of(lines_ref[...], weights_ref, points_ref, cells_ref.shape[2])):
        cells_ref[j] = cell


def second_kernel(steps, me_ref, lines_ref, weights_ref, points_ref, cells_ref, codes_ref, body_ref, packed_ref):
    nwide, rows, lanes = body_ref.shape
    for o in range(nwide):
        packed_ref[o, :rows, :] = body_ref[o]
    early = cells_ref.shape[0]
    cells = [cells_ref[j] for j in range(early)]
    cells += cells_of(lines_ref[...], weights_ref, points_ref, lanes)
    for j, cell in enumerate(cells):
        owner = me_ref[0] ^ steps[j]
        packed_ref[owner, rows:, :] = (codes_ref[owner] + cell).astype(BF16)


def first_sums(lines, weights, points, lanes):
    owned = weights.shape[2]
    devices = lines.shape[0] // 2
    pairs = devices * lines.shape[1] * owned
    vmem = pl.BlockSpec(memory_space=pltpu.VMEM)
    return pl.pallas_call(
        first_kernel,
        out_shape=jax.ShapeDtypeStruct((devices, 2 * HARM, lanes), F32),
        in_specs=[vmem] * 3,
        out_specs=vmem,
        compiler_params=pltpu.CompilerParams(vmem_limit_bytes=40 * 2**20),
        cost_estimate=pl.CostEstimate(flops=pairs * 2000, bytes_accessed=owned * 70, transcendentals=pairs),
    )(lines, weights, points)


def second_sums(lines, weights, points, cells, codes, body, steps):
    owned = weights.shape[2]
    nwide, rows, lanes = body.shape
    pairs = lines.shape[0] // 2 * lines.shape[1] * owned
    vmem = pl.BlockSpec(memory_space=pltpu.VMEM)
    me = lax.axis_index("wide").reshape(1)

    def kernel(*refs):
        second_kernel(steps, *refs)

    return pl.pallas_call(
        kernel,
        out_shape=jax.ShapeDtypeStruct((nwide, rows + 8, lanes), BF16),
        in_specs=[pl.BlockSpec(memory_space=pltpu.SMEM)] + [vmem] * 6,
        out_specs=vmem,
        compiler_params=pltpu.CompilerParams(vmem_limit_bytes=40 * 2**20),
        cost_estimate=pl.CostEstimate(flops=pairs * 2000, bytes_accessed=owned * 70, transcendentals=pairs),
    )(me, lines, weights, points, cells, codes, body)


def swap(x, nwide, bit):
    return lax.ppermute(x, "wide", [(i, i ^ bit) for i in range(nwide)])


def shards(flow, positions, normals, panel_ids, observers):
    owned = flow.shape[2]
    nwide = lax.axis_size("wide")
    listeners = observers.shape[1]
    near = nwide // 4
    others = [swap(observers, nwide, n) for n in range(1, near)]
    spectra, weights, points, ids, mine = sources(flow, normals, positions, panel_ids, observers)
    others, spectra = lax.optimization_barrier((others, spectra))
    lines = jnp.concatenate([mine] + others, axis=0)
    other = swap(lines, nwide, near)
    packed, codes = pack(spectra, ids, nwide)
    other, packed = lax.optimization_barrier((other, packed))
    lines = jnp.concatenate([lines, other], axis=0)
    other = swap(lines, nwide, 2 * near)
    cells = first_sums(lines, weights, points, packed.shape[2])
    other, cells = lax.optimization_barrier((other, cells))
    steps = [n ^ z for z in range(0, 4 * near, near) for n in range(near)]
    packed = second_sums(other, weights, points, cells, codes, packed, steps)
    received = lax.all_to_all(packed, "wide", split_axis=0, concat_axis=0, tiled=True)
    panel_spectra, pressure = place(received, owned, listeners)
    return (panel_spectra, pressure.T)


def solution(mesh):
    placed = (
        P(None, None, ("case", "wide")),
        P(None, ("case", "wide")),
        P(None, ("case", "wide")),
        P(("case", "wide")),
        P(None, ("case", "wide")),
    )
    return jax.shard_map(
        shards,
        mesh=mesh,
        in_specs=placed,
        out_specs=(P(None, ("case", "wide")), P(("case", "wide"), None)),
        check_vma=False,
    )
```

```python
import math

import jax
import jax.numpy as jnp
import numpy as np
from jax import lax
from jax.experimental import pallas as pl
from jax.experimental.pallas import tpu as pltpu
from jax.sharding import PartitionSpec as P

NT = 16
HARM = 4
ROWS = 8 * HARM
WAVENUMBER = 2.0
GROUND = 3.0
LOW = 256
F32 = jnp.float32
BF16 = jnp.bfloat16
NT_DIMS = (((1,), (1,)), ((), ()))


def fit(function, degree):
    nodes = np.cos(np.pi * (np.arange(64) + 0.5) / 64) * 0.5
    squares = nodes * nodes
    powers = np.stack([squares**d for d in range(degree + 1)], axis=1)
    return [float(c) for c in np.linalg.lstsq(powers, function(nodes), rcond=None)[0]]


TURN = WAVENUMBER / (2.0 * math.pi)
HALF_SINE = fit(lambda f: math.sqrt(2.0) * (1.0 - 1e-6) * np.sin(np.pi * f) / f, 4)


def horner(coefficients, x):
    value = coefficients[-1]
    for c in coefficients[-2::-1]:
        value = value * x + c
    return value


def thirds(x):
    first = x.astype(BF16).astype(F32)
    second = (x - first).astype(BF16).astype(F32)
    return [first, second, x - first - second]


def dft_split():
    samples = np.arange(NT)[:, None]
    harmonic = np.arange(1, HARM + 1)[None, :]
    angle = 2.0 * np.pi / NT * samples * harmonic
    table = np.stack([np.cos(angle), -np.sin(angle)], axis=2) * (2.0 / NT)
    table = table.reshape(NT, 2 * HARM).T
    block = np.kron(np.eye(4), table).astype(np.float32)
    order = [8 * a + 2 * h + c for h in range(HARM) for a in range(4) for c in range(2)]
    block = np.concatenate([block, block[order]], axis=0)
    high = block.astype(jnp.bfloat16)
    low = (block - high.astype(np.float32)).astype(jnp.bfloat16)
    return np.concatenate([high, high, low, low], axis=1)


def pack_shape(nwide, owned):
    capacity = 2 * owned // nwide
    lanes = min(capacity, 128)
    subs = capacity // lanes
    return capacity, lanes, subs, ROWS * subs + 8


def source_kernel(
    flow_hbm, normals_hbm, place_hbm, table_hbm, ids_hbm, over_hbm,
    spectra_ref, weights_ref, points_ref, ids_ref, mine_ref,
    flow_ref, normals_ref, place_ref, table_ref, sems,
):
    owned = flow_ref.shape[2]
    step = min(256, owned)
    pieces = 4
    wide = owned // pieces
    copies = [
        pltpu.make_async_copy(normals_hbm, normals_ref, sems.at[0]),
        pltpu.make_async_copy(place_hbm, place_ref, sems.at[1]),
        pltpu.make_async_copy(table_hbm, table_ref, sems.at[2]),
    ]
    passed = [
        pltpu.make_async_copy(ids_hbm, ids_ref, sems.at[3]),
        pltpu.make_async_copy(over_hbm, mine_ref, sems.at[4]),
    ]
    flows = [
        pltpu.make_async_copy(
            flow_hbm.at[:, :, wide * p : wide * p + wide], flow_ref.at[:, :, wide * p : wide * p + wide], sems.at[5 + p]
        )
        for p in range(pieces)
    ]
    for copy in copies + flows + passed:
        copy.start()
    for copy in copies:
        copy.wait()
    table = table_ref[...]
    scale = TURN * TURN
    for start in range(0, owned, step):
        cols = slice(start, start + step)
        place = place_ref[:, cols].astype(F32)
        px, py, pz = place[0:1], place[1:2], place[2:3]
        here = scale * (px * px + py * py + pz * pz + (2.0 * GROUND) * pz)
        one, none = jnp.ones_like(here), jnp.zeros_like(here)
        points = jnp.concatenate([px] * 3 + [py] * 3 + [one] * 3 + thirds(here) + [none] * 4, axis=0)
        points_ref[cols, :] = points.T.astype(BF16)
    for start in range(0, owned, step):
        if start % wide == 0:
            flows[start // wide].wait()
        cols = slice(start, start + step)
        normal = normals_ref[:, cols].astype(F32)
        n0, n1, n2 = normal[0:1], normal[1:2], normal[2:3]
        density = 1.0 + 0.2 * flow_ref[0, :, cols].astype(F32)
        v0 = 0.5 * flow_ref[1, :, cols].astype(F32)
        v1 = 0.5 * flow_ref[2, :, cols].astype(F32)
        v2 = 0.5 * flow_ref[3, :, cols].astype(F32)
        fluct = flow_ref[4, :, cols].astype(F32)
        across = v0 * n0 + v1 * n1 + v2 * n2
        source = density * across
        parts = jnp.concatenate(
            [source, fluct * n0 + v0 * source, fluct * n1 + v1 * source, fluct * n2 + v2 * source], axis=0
        )
        top = parts.astype(BF16)
        rest = (parts - top.astype(F32)).astype(BF16)
        both = jnp.concatenate([top, rest, top, rest], axis=0)
        spectra = jnp.dot(table, both, preferred_element_type=F32).astype(BF16)
        spectra_ref[:, cols] = spectra[:ROWS]
        by_harmonic = spectra[ROWS:].astype(F32)
        place = place_ref[:, cols].astype(F32)
        px, py, pz = place[0:1], place[1:2], place[2:3]
        down = pz + GROUND
        none = jnp.zeros_like(px)
        factors = jnp.concatenate([none, none, px, px, py, py, down, down], axis=0)
        for h in range(HARM):
            group = by_harmonic[8 * h : 8 * h + 8]
            shares = group * factors
            along = -(shares[2:4] + shares[4:6] + shares[6:8])
            along_high = along.astype(BF16).astype(F32)
            weights_ref[h, :, cols] = jnp.concatenate(
                [group, along_high, along - along_high, jnp.zeros((4, step), F32)], axis=0
            ).astype(BF16)
    for copy in passed:
        copy.wait()


def sources(flow, normals, positions, ids, observers):
    owned = flow.shape[2]
    vmem = pl.BlockSpec(memory_space=pltpu.VMEM)
    anywhere = pl.BlockSpec(memory_space=pl.ANY)
    table = jnp.asarray(dft_split())
    arrays = (flow, normals, positions, table, ids.reshape(1, owned), observers)
    return pl.pallas_call(
        source_kernel,
        out_shape=(
            jax.ShapeDtypeStruct((ROWS, owned), BF16),
            jax.ShapeDtypeStruct((HARM, 16, owned), BF16),
            jax.ShapeDtypeStruct((owned, 16), BF16),
            jax.ShapeDtypeStruct((1, owned), jnp.int32),
            jax.ShapeDtypeStruct(observers.shape, F32),
        ),
        in_specs=[anywhere] * 6,
        out_specs=(vmem,) * 5,
        scratch_shapes=[
            pltpu.VMEM(flow.shape, BF16),
            pltpu.VMEM(normals.shape, BF16),
            pltpu.VMEM(positions.shape, BF16),
            pltpu.VMEM(table.shape, BF16),
            pltpu.SemaphoreType.DMA((9,)),
        ],
        compiler_params=pltpu.CompilerParams(vmem_limit_bytes=32 * 2**20),
    )(*(pltpu.with_memory_space_constraint(x, pltpu.HBM) for x in arrays))


def pack_kernel(nwide, spectra_ref, ids_ref, packed_ref, codes_ref, left, right):
    owned = spectra_ref.shape[1]
    capacity, lanes, subs, _ = pack_shape(nwide, owned)
    step = min(256, owned)
    upper = (
        lax.broadcasted_iota(jnp.int32, (step, step), 0)
        < lax.broadcasted_iota(jnp.int32, (step, step), 1)
    ).astype(F32).astype(BF16)
    ids = ids_ref[...]
    owner = ids // owned
    local = ids - owner * owned
    high = local // LOW
    code_high = (high + 1).astype(F32)
    code_low = (local - high * LOW).astype(F32)
    carry = jnp.zeros((nwide, 1), F32)
    which = lax.broadcasted_iota(jnp.int32, (nwide, step), 0)
    slots = lax.broadcasted_iota(jnp.int32, (capacity, step), 0).astype(F32)
    codes_row = lax.broadcasted_iota(jnp.int32, (8, step), 0)
    for start in range(0, owned, step):
        cols = slice(start, start + step)
        own = which == owner[:, cols]
        ownf = own.astype(F32)
        before = jnp.dot(ownf.astype(BF16), upper, preferred_element_type=F32) + carry
        rank = jnp.sum(before * ownf, axis=0, keepdims=True)
        carry = before[:, step - 1 : step] + ownf[:, step - 1 : step]
        right[:, cols] = (slots == rank).astype(F32).astype(BF16)
        codes = jnp.where(codes_row == 0, code_high[:, cols], jnp.where(codes_row == 1, code_low[:, cols], 0.0))
        codes = jnp.concatenate([codes, jnp.zeros_like(codes)], axis=0).astype(BF16)
        values = jnp.concatenate([spectra_ref[:, cols], codes], axis=0)
        for o in range(nwide):
            left[48 * o : 48 * o + 48, cols] = jnp.where(owner[:, cols] == o, values, jnp.zeros_like(values))
    packed = lax.dot_general(left[...], right[...], NT_DIMS, preferred_element_type=F32)
    lane = lax.broadcasted_iota(jnp.int32, (8, lanes), 1)
    for o in range(nwide):
        block = packed[48 * o : 48 * o + 48]
        for s in range(subs):
            packed_ref[o, ROWS * s : ROWS * s + ROWS, :] = block[:ROWS, lanes * s : lanes * s + lanes].astype(BF16)
        codes = []
        for s in range(subs):
            upper_half = block[ROWS : ROWS + 8, lanes * s : lanes * s + lanes]
            lower_half = jnp.concatenate([upper_half[:, lanes // 2 :], upper_half[:, : lanes // 2]], axis=1)
            codes += [lower_half[:2], upper_half[:2]]
        codes = jnp.concatenate(codes + [jnp.zeros((8 - 4 * subs, lanes), F32)] * (subs == 1), axis=0)
        codes_ref[o] = jnp.where(lane < lanes // 2, 0.0, codes)


def pack(spectra, ids, nwide):
    owned = spectra.shape[1]
    capacity, lanes, subs, _ = pack_shape(nwide, owned)
    vmem = pl.BlockSpec(memory_space=pltpu.VMEM)

    def body(*refs):
        pack_kernel(nwide, *refs)

    return pl.pallas_call(
        body,
        out_shape=(
            jax.ShapeDtypeStruct((nwide, ROWS * subs, lanes), BF16),
            jax.ShapeDtypeStruct((nwide, 8, lanes), F32),
        ),
        in_specs=[vmem] * 2,
        out_specs=(vmem, vmem),
        scratch_shapes=[
            pltpu.VMEM((48 * nwide, owned), BF16),
            pltpu.VMEM((capacity, owned), BF16),
        ],
        compiler_params=pltpu.CompilerParams(vmem_limit_bytes=40 * 2**20),
    )(spectra, ids)


def place_kernel(scale, received_ref, spectra_ref, pressure_ref):
    nwide, depth, lanes = received_ref.shape
    owned = spectra_ref.shape[1]
    listeners = pressure_ref.shape[1]
    subs = (depth - 8) // ROWS
    heights = owned // LOW
    group = max(1, 256 // (lanes * subs))
    width = lanes * subs * group
    lows = lax.broadcasted_iota(jnp.int32, (LOW, width), 0).astype(F32)
    total = jnp.zeros((heights * ROWS, LOW), F32)
    sums = jnp.zeros((2 * HARM, lanes), F32)
    lower = lax.broadcasted_iota(jnp.int32, (1, lanes), 1) < lanes // 2
    for first in range(0, nwide, group):
        blocks, high, low = [], [], []
        for o in range(first, first + group):
            codes = received_ref[o, ROWS * subs : ROWS * subs + 8, :].astype(F32)
            sums = sums + codes
            turned = jnp.concatenate([codes[:, lanes // 2 :], codes[:, : lanes // 2]], axis=1)
            for s in range(subs):
                blocks.append(received_ref[o, ROWS * s : ROWS * s + ROWS, :])
                high.append(jnp.where(lower, turned[4 * s : 4 * s + 1], codes[4 * s + 2 : 4 * s + 3]))
                low.append(jnp.where(lower, turned[4 * s + 1 : 4 * s + 2], codes[4 * s + 3 : 4 * s + 4]))
        values = jnp.concatenate(blocks, axis=1)
        high = jnp.concatenate(high, axis=1)
        low = jnp.concatenate(low, axis=1)
        spread = (lows == low).astype(F32).astype(BF16)
        picked = jnp.concatenate(
            [jnp.where(high == h + 1.0, values, jnp.zeros_like(values)) for h in range(heights)], axis=0
        )
        total = total + lax.dot_general(picked, spread, NT_DIMS, preferred_element_type=F32)
    for h in range(heights):
        spectra_ref[:, LOW * h : LOW * h + LOW] = total[ROWS * h : ROWS * h + ROWS].astype(BF16)
    pressure_ref[...] = scale * (sums[:, listeners : 2 * listeners] + sums[:, :listeners])


def place(received, owned, listeners):
    nwide = received.shape[0]
    vmem = pl.BlockSpec(memory_space=pltpu.VMEM)
    scale = 2.0 / math.sqrt(owned * nwide)

    def body(*refs):
        place_kernel(scale, *refs)

    return pl.pallas_call(
        body,
        out_shape=(
            jax.ShapeDtypeStruct((ROWS, owned), BF16),
            jax.ShapeDtypeStruct((2 * HARM, listeners), F32),
        ),
        in_specs=[vmem],
        out_specs=(vmem, vmem),
        compiler_params=pltpu.CompilerParams(vmem_limit_bytes=40 * 2**20),
    )(received)


SUB = 128
KINDS = 3


def pair_sums(lines, weights_ref, points_ref):
    owned = weights_ref.shape[2]
    count = lines.shape[0] // 2
    listeners = lines.shape[1]
    step = min(256, owned)
    scale = TURN * TURN
    over_x = jnp.concatenate([lines[2 * j : 2 * j + 1] for j in range(count)], axis=1)
    over_y = jnp.concatenate([lines[2 * j + 1 : 2 * j + 2] for j in range(count)], axis=1)
    there = scale * (over_x * over_x + over_y * over_y + GROUND * GROUND)
    one, zero = jnp.ones_like(there), jnp.zeros_like(there)
    views = jnp.concatenate(
        thirds((-2.0 * scale) * over_x) + thirds((-2.0 * scale) * over_y) + thirds(there) + [one] * 3 + [zero] * 4,
        axis=0,
    ).astype(BF16)
    width = min(128, count * listeners)
    made = []
    for left in range(0, count * listeners, width):
        view = views[:, left : left + width]
        totals = [[None] * KINDS for _ in range(HARM)]
        pending = []

        def drain(number):
            for _ in range(min(number, len(pending))):
                h, m, begin, pieces = pending.pop(0)
                whole = pieces[0] if len(pieces) == 1 else jnp.concatenate(pieces, axis=0)
                part = weights_ref[h, :, begin : begin + step]
                product = jnp.dot(part, whole, preferred_element_type=F32)
                totals[h][m] = product if totals[h][m] is None else totals[h][m] + product

        for start in range(0, owned, step):
            mats = [[[] for _ in range(KINDS)] for _ in range(HARM)]
            for row in range(start, start + step, SUB):
                square = jnp.dot(points_ref[row : row + SUB, :], view, preferred_element_type=F32)
                inv = lax.rsqrt(square)
                turns = square * inv
                frac = turns - jnp.round(turns)
                half = horner(HALF_SINE, frac * frac) * frac
                versine = half * half
                cosine = 1.0 - versine
                twoc = cosine + cosine
                rest = 2.0 - versine
                inv_bf = inv.astype(BF16)
                c_prev, s_prev = inv, None
                c_now = inv * cosine
                s_now = (inv * half) * (rest * lax.rsqrt(rest))
                for h in range(HARM):
                    c_bf, s_bf = c_now.astype(BF16), s_now.astype(BF16)
                    d, e = (inv * c_now).astype(BF16), (inv * s_now).astype(BF16)
                    for m, pair in enumerate(((c_bf, s_bf), (d, e), (inv_bf * d, inv_bf * e))):
                        mats[h][m].append(jnp.concatenate(pair, axis=1))
                    if h < HARM - 1:
                        c_next = twoc * c_now - c_prev
                        s_next = twoc * s_now - s_prev if h else twoc * s_now
                        c_prev, s_prev, c_now, s_now = c_now, s_now, c_next, s_next
                drain(HARM * KINDS * SUB // step)
            drain(HARM * KINDS)
            pending += [(h, m, start, mats[h][m]) for h in range(HARM) for m in range(KINDS)]
        drain(HARM * KINDS)
        ox, oy = over_x[:, left : left + width], over_y[:, left : left + width]
        rows = []
        for h in range(HARM):
            wavenum = WAVENUMBER * (h + 1)
            totals[h] = [half for both in totals[h] for half in (both[:, :width], both[:, width:])]
            cos_sum, sin_sum = totals[h][0], totals[h][1]

            def loads(m):
                t = totals[h][m]
                return [
                    ox * t[2 + c : 3 + c] + oy * t[4 + c : 5 + c] + (t[8 + c : 9 + c] + t[10 + c : 11 + c])
                    for c in (0, 1)
                ]

            (dr, di), (er, ei), (ur, ui), (vr, vi) = loads(2), loads(3), loads(4), loads(5)
            real = wavenum * (er - di) + TURN * (ur + vi)
            imag = wavenum * (ei + dr) + TURN * (ui - vr)
            rows.append(TURN * (wavenum * (sin_sum[0:1] - cos_sum[1:2]) + TURN * real))
            rows.append(TURN * (wavenum * (cos_sum[0:1] + sin_sum[1:2]) + TURN * imag))
        made.append(jnp.concatenate(rows, axis=0))
    return made


def cells_of(lines, weights_ref, points_ref, lanes):
    listeners = lines.shape[1]
    cells = []
    for value in pair_sums(lines, weights_ref, points_ref):
        top = value.astype(BF16).astype(F32)
        split = [top, value - top]
        for j in range(value.shape[1] // listeners):
            cell = [half[:, listeners * j : listeners * j + listeners] for half in split]
            cell.append(jnp.zeros((2 * HARM, lanes - 2 * listeners), F32))
            cells.append(jnp.concatenate(cell, axis=1))
    return cells


def first_kernel(lines_ref, weights_ref, points_ref, cells_ref):
    for j, cell in enumerate(cells_of(lines_ref[...], weights_ref, points_ref, cells_ref.shape[2])):
        cells_ref[j] = cell


def second_kernel(steps, me_ref, lines_ref, weights_ref, points_ref, cells_ref, codes_ref, body_ref, packed_ref):
    nwide, rows, lanes = body_ref.shape
    for o in range(nwide):
        packed_ref[o, :rows, :] = body_ref[o]
    early = cells_ref.shape[0]
    cells = [cells_ref[j] for j in range(early)]
    cells += cells_of(lines_ref[...], weights_ref, points_ref, lanes)
    for j, cell in enumerate(cells):
        owner = me_ref[0] ^ steps[j]
        packed_ref[owner, rows:, :] = (codes_ref[owner] + cell).astype(BF16)


def first_sums(lines, weights, points, lanes):
    owned = weights.shape[2]
    devices = lines.shape[0] // 2
    pairs = devices * lines.shape[1] * owned
    vmem = pl.BlockSpec(memory_space=pltpu.VMEM)
    return pl.pallas_call(
        first_kernel,
        out_shape=jax.ShapeDtypeStruct((devices, 2 * HARM, lanes), F32),
        in_specs=[vmem] * 3,
        out_specs=vmem,
        compiler_params=pltpu.CompilerParams(vmem_limit_bytes=40 * 2**20),
        cost_estimate=pl.CostEstimate(flops=pairs * 2000, bytes_accessed=owned * 70, transcendentals=pairs),
    )(lines, weights, points)


def second_sums(lines, weights, points, cells, codes, body, steps):
    owned = weights.shape[2]
    nwide, rows, lanes = body.shape
    pairs = lines.shape[0] // 2 * lines.shape[1] * owned
    vmem = pl.BlockSpec(memory_space=pltpu.VMEM)
    me = lax.axis_index("wide").reshape(1)

    def kernel(*refs):
        second_kernel(steps, *refs)

    return pl.pallas_call(
        kernel,
        out_shape=jax.ShapeDtypeStruct((nwide, rows + 8, lanes), BF16),
        in_specs=[pl.BlockSpec(memory_space=pltpu.SMEM)] + [vmem] * 6,
        out_specs=vmem,
        compiler_params=pltpu.CompilerParams(vmem_limit_bytes=40 * 2**20),
        cost_estimate=pl.CostEstimate(flops=pairs * 2000, bytes_accessed=owned * 70, transcendentals=pairs),
    )(me, lines, weights, points, cells, codes, body)


def swap(x, nwide, bit):
    return lax.ppermute(x, "wide", [(i, i ^ bit) for i in range(nwide)])


def shards(flow, positions, normals, panel_ids, observers):
    owned = flow.shape[2]
    nwide = lax.axis_size("wide")
    listeners = observers.shape[1]
    near = nwide // 4
    others = [swap(observers, nwide, n) for n in range(1, near)]
    spectra, weights, points, ids, mine = sources(flow, normals, positions, panel_ids, observers)
    others, spectra = lax.optimization_barrier((others, spectra))
    lines = jnp.concatenate([mine] + others, axis=0)
    other = swap(lines, nwide, near)
    packed, codes = pack(spectra, ids, nwide)
    other, packed = lax.optimization_barrier((other, packed))
    lines = jnp.concatenate([lines, other], axis=0)
    other = swap(lines, nwide, 2 * near)
    cells = first_sums(lines, weights, points, packed.shape[2])
    other, cells = lax.optimization_barrier((other, cells))
    steps = [n ^ z for z in range(0, 4 * near, near) for n in range(near)]
    packed = second_sums(other, weights, points, cells, codes, packed, steps)
    received = lax.all_to_all(packed, "wide", split_axis=0, concat_axis=0, tiled=True)
    panel_spectra, pressure = place(received, owned, listeners)
    return (panel_spectra, pressure.T)


def solution(mesh):
    placed = (
        P(None, None, ("case", "wide")),
        P(None, ("case", "wide")),
        P(None, ("case", "wide")),
        P(("case", "wide")),
        P(None, ("case", "wide")),
    )
    return jax.shard_map(
        shards,
        mesh=mesh,
        in_specs=placed,
        out_specs=(P(None, ("case", "wide")), P(("case", "wide"), None)),
        check_vma=False,
    )
```

```python
import math

import jax
import jax.numpy as jnp
import numpy as np
from jax import lax
from jax.experimental import pallas as pl
from jax.experimental.pallas import tpu as pltpu
from jax.sharding import PartitionSpec as P

NT = 16
HARM = 4
ROWS = 8 * HARM
WAVENUMBER = 2.0
GROUND = 3.0
LOW = 256
F32 = jnp.float32
BF16 = jnp.bfloat16
NT_DIMS = (((1,), (1,)), ((), ()))


def fit(function, degree):
    nodes = np.cos(np.pi * (np.arange(64) + 0.5) / 64) * 0.5
    squares = nodes * nodes
    powers = np.stack([squares**d for d in range(degree + 1)], axis=1)
    return [float(c) for c in np.linalg.lstsq(powers, function(nodes), rcond=None)[0]]


TURN = WAVENUMBER / (2.0 * math.pi)
HALF_SINE = fit(lambda f: math.sqrt(2.0) * np.sin(np.pi * f) / f, 4)


def horner(coefficients, x):
    value = coefficients[-1]
    for c in coefficients[-2::-1]:
        value = value * x + c
    return value


def thirds(x):
    first = x.astype(BF16).astype(F32)
    second = (x - first).astype(BF16).astype(F32)
    return [first, second, x - first - second]


def dft_split():
    samples = np.arange(NT)[:, None]
    harmonic = np.arange(1, HARM + 1)[None, :]
    angle = 2.0 * np.pi / NT * samples * harmonic
    table = np.stack([np.cos(angle), -np.sin(angle)], axis=2) * (2.0 / NT)
    table = table.reshape(NT, 2 * HARM).T
    block = np.kron(np.eye(4), table).astype(np.float32)
    order = [8 * a + 2 * h + c for h in range(HARM) for a in range(4) for c in range(2)]
    block = np.concatenate([block, block[order]], axis=0)
    high = block.astype(jnp.bfloat16)
    low = (block - high.astype(np.float32)).astype(jnp.bfloat16)
    return np.concatenate([high, high, low, low], axis=1)


def pack_shape(nwide, owned):
    capacity = 2 * owned // nwide
    lanes = min(capacity, 128)
    subs = capacity // lanes
    return capacity, lanes, subs, ROWS * subs + 8


def source_kernel(
    flow_hbm, normals_hbm, place_hbm, table_hbm, ids_hbm, over_hbm,
    spectra_ref, weights_ref, points_ref, ids_ref, mine_ref,
    flow_ref, normals_ref, place_ref, table_ref, sems,
):
    owned = flow_ref.shape[2]
    step = min(256, owned)
    copies = [
        pltpu.make_async_copy(normals_hbm, normals_ref, sems.at[0]),
        pltpu.make_async_copy(place_hbm, place_ref, sems.at[1]),
        pltpu.make_async_copy(table_hbm, table_ref, sems.at[2]),
        pltpu.make_async_copy(flow_hbm, flow_ref, sems.at[5]),
    ]
    passed = [
        pltpu.make_async_copy(ids_hbm, ids_ref, sems.at[3]),
        pltpu.make_async_copy(over_hbm, mine_ref, sems.at[4]),
    ]
    for copy in copies + passed:
        copy.start()
    for copy in copies:
        copy.wait()
    table = table_ref[...]
    scale = TURN * TURN
    for start in range(0, owned, step):
        cols = slice(start, start + step)
        normal = normals_ref[:, cols].astype(F32)
        n0, n1, n2 = normal[0:1], normal[1:2], normal[2:3]
        density = 1.0 + 0.2 * flow_ref[0, :, cols].astype(F32)
        v0 = 0.5 * flow_ref[1, :, cols].astype(F32)
        v1 = 0.5 * flow_ref[2, :, cols].astype(F32)
        v2 = 0.5 * flow_ref[3, :, cols].astype(F32)
        fluct = flow_ref[4, :, cols].astype(F32)
        across = v0 * n0 + v1 * n1 + v2 * n2
        source = density * across
        parts = jnp.concatenate(
            [source, fluct * n0 + v0 * source, fluct * n1 + v1 * source, fluct * n2 + v2 * source], axis=0
        )
        top = parts.astype(BF16)
        rest = (parts - top.astype(F32)).astype(BF16)
        both = jnp.concatenate([top, rest, top, rest], axis=0)
        spectra = jnp.dot(table, both, preferred_element_type=F32).astype(BF16)
        spectra_ref[:, cols] = spectra[:ROWS]
        by_harmonic = spectra[ROWS:].astype(F32)
        place = place_ref[:, cols].astype(F32)
        px, py, pz = place[0:1], place[1:2], place[2:3]
        down = pz + GROUND
        none = jnp.zeros_like(px)
        factors = jnp.concatenate([none, none, px, px, py, py, down, down], axis=0)
        for h in range(HARM):
            group = by_harmonic[8 * h : 8 * h + 8]
            shares = group * factors
            along = -(shares[2:4] + shares[4:6] + shares[6:8])
            along_high = along.astype(BF16).astype(F32)
            weights_ref[h, :, cols] = jnp.concatenate(
                [group, along_high, along - along_high, jnp.zeros((4, step), F32)], axis=0
            ).astype(BF16)
        here = scale * (px * px + py * py + pz * pz + (2.0 * GROUND) * pz)
        one = jnp.ones_like(here)
        points = jnp.concatenate([px] * 3 + [py] * 3 + [one] * 3 + thirds(here) + [none] * 4, axis=0)
        points_ref[cols, :] = points.T.astype(BF16)
    for copy in passed:
        copy.wait()


def sources(flow, normals, positions, ids, observers):
    owned = flow.shape[2]
    vmem = pl.BlockSpec(memory_space=pltpu.VMEM)
    anywhere = pl.BlockSpec(memory_space=pl.ANY)
    table = jnp.asarray(dft_split())
    arrays = (flow, normals, positions, table, ids.reshape(1, owned), observers)
    return pl.pallas_call(
        source_kernel,
        out_shape=(
            jax.ShapeDtypeStruct((ROWS, owned), BF16),
            jax.ShapeDtypeStruct((HARM, 16, owned), BF16),
            jax.ShapeDtypeStruct((owned, 16), BF16),
            jax.ShapeDtypeStruct((1, owned), jnp.int32),
            jax.ShapeDtypeStruct(observers.shape, F32),
        ),
        in_specs=[anywhere] * 6,
        out_specs=(vmem,) * 5,
        scratch_shapes=[
            pltpu.VMEM(flow.shape, BF16),
            pltpu.VMEM(normals.shape, BF16),
            pltpu.VMEM(positions.shape, BF16),
            pltpu.VMEM(table.shape, BF16),
            pltpu.SemaphoreType.DMA((6,)),
        ],
        compiler_params=pltpu.CompilerParams(vmem_limit_bytes=32 * 2**20),
    )(*(pltpu.with_memory_space_constraint(x, pltpu.HBM) for x in arrays))


def pack_kernel(nwide, spectra_ref, ids_ref, packed_ref, codes_ref, left, right):
    owned = spectra_ref.shape[1]
    capacity, lanes, subs, _ = pack_shape(nwide, owned)
    step = min(256, owned)
    upper = (
        lax.broadcasted_iota(jnp.int32, (step, step), 0)
        < lax.broadcasted_iota(jnp.int32, (step, step), 1)
    ).astype(F32).astype(BF16)
    ids = ids_ref[...]
    owner = ids // owned
    local = ids - owner * owned
    high = local // LOW
    code_high = (high + 1).astype(F32)
    code_low = (local - high * LOW).astype(F32)
    carry = jnp.zeros((nwide, 1), F32)
    which = lax.broadcasted_iota(jnp.int32, (nwide, step), 0)
    slots = lax.broadcasted_iota(jnp.int32, (capacity, step), 0).astype(F32)
    codes_row = lax.broadcasted_iota(jnp.int32, (8, step), 0)
    for start in range(0, owned, step):
        cols = slice(start, start + step)
        own = which == owner[:, cols]
        ownf = own.astype(F32)
        before = jnp.dot(ownf.astype(BF16), upper, preferred_element_type=F32) + carry
        rank = jnp.sum(before * ownf, axis=0, keepdims=True)
        carry = before[:, step - 1 : step] + ownf[:, step - 1 : step]
        right[:, cols] = (slots == rank).astype(F32).astype(BF16)
        codes = jnp.where(codes_row == 0, code_high[:, cols], jnp.where(codes_row == 1, code_low[:, cols], 0.0))
        codes = jnp.concatenate([codes, jnp.zeros_like(codes)], axis=0).astype(BF16)
        values = jnp.concatenate([spectra_ref[:, cols], codes], axis=0)
        for o in range(nwide):
            left[48 * o : 48 * o + 48, cols] = jnp.where(owner[:, cols] == o, values, jnp.zeros_like(values))
    packed = lax.dot_general(left[...], right[...], NT_DIMS, preferred_element_type=F32)
    lane = lax.broadcasted_iota(jnp.int32, (8, lanes), 1)
    for o in range(nwide):
        block = packed[48 * o : 48 * o + 48]
        for s in range(subs):
            packed_ref[o, ROWS * s : ROWS * s + ROWS, :] = block[:ROWS, lanes * s : lanes * s + lanes].astype(BF16)
        codes = []
        for s in range(subs):
            upper_half = block[ROWS : ROWS + 8, lanes * s : lanes * s + lanes]
            lower_half = jnp.concatenate([upper_half[:, lanes // 2 :], upper_half[:, : lanes // 2]], axis=1)
            codes += [lower_half[:2], upper_half[:2]]
        codes = jnp.concatenate(codes + [jnp.zeros((8 - 4 * subs, lanes), F32)] * (subs == 1), axis=0)
        codes_ref[o] = jnp.where(lane < lanes // 2, 0.0, codes)


def pack(spectra, ids, nwide):
    owned = spectra.shape[1]
    capacity, lanes, subs, _ = pack_shape(nwide, owned)
    vmem = pl.BlockSpec(memory_space=pltpu.VMEM)

    def body(*refs):
        pack_kernel(nwide, *refs)

    return pl.pallas_call(
        body,
        out_shape=(
            jax.ShapeDtypeStruct((nwide, ROWS * subs, lanes), BF16),
            jax.ShapeDtypeStruct((nwide, 8, lanes), F32),
        ),
        in_specs=[vmem] * 2,
        out_specs=(vmem, vmem),
        scratch_shapes=[
            pltpu.VMEM((48 * nwide, owned), BF16),
            pltpu.VMEM((capacity, owned), BF16),
        ],
        compiler_params=pltpu.CompilerParams(vmem_limit_bytes=40 * 2**20),
    )(spectra, ids)


def place_kernel(scale, received_ref, spectra_ref, pressure_ref):
    nwide, depth, lanes = received_ref.shape
    owned = spectra_ref.shape[1]
    listeners = pressure_ref.shape[1]
    subs = (depth - 8) // ROWS
    heights = owned // LOW
    group = max(1, 256 // (lanes * subs))
    width = lanes * subs * group
    lows = lax.broadcasted_iota(jnp.int32, (LOW, width), 0).astype(F32)
    total = jnp.zeros((heights * ROWS, LOW), F32)
    sums = jnp.zeros((2 * HARM, lanes), F32)
    lower = lax.broadcasted_iota(jnp.int32, (1, lanes), 1) < lanes // 2
    for first in range(0, nwide, group):
        blocks, high, low = [], [], []
        for o in range(first, first + group):
            codes = received_ref[o, ROWS * subs : ROWS * subs + 8, :].astype(F32)
            sums = sums + codes
            turned = jnp.concatenate([codes[:, lanes // 2 :], codes[:, : lanes // 2]], axis=1)
            for s in range(subs):
                blocks.append(received_ref[o, ROWS * s : ROWS * s + ROWS, :])
                high.append(jnp.where(lower, turned[4 * s : 4 * s + 1], codes[4 * s + 2 : 4 * s + 3]))
                low.append(jnp.where(lower, turned[4 * s + 1 : 4 * s + 2], codes[4 * s + 3 : 4 * s + 4]))
        values = jnp.concatenate(blocks, axis=1)
        high = jnp.concatenate(high, axis=1)
        low = jnp.concatenate(low, axis=1)
        spread = (lows == low).astype(F32).astype(BF16)
        picked = jnp.concatenate(
            [jnp.where(high == h + 1.0, values, jnp.zeros_like(values)) for h in range(heights)], axis=0
        )
        total = total + lax.dot_general(picked, spread, NT_DIMS, preferred_element_type=F32)
    for h in range(heights):
        spectra_ref[:, LOW * h : LOW * h + LOW] = total[ROWS * h : ROWS * h + ROWS].astype(BF16)
    pressure_ref[...] = scale * (sums[:, listeners : 2 * listeners] + sums[:, :listeners])


def place(received, owned, listeners):
    nwide = received.shape[0]
    vmem = pl.BlockSpec(memory_space=pltpu.VMEM)
    scale = 2.0 / math.sqrt(owned * nwide)

    def body(*refs):
        place_kernel(scale, *refs)

    return pl.pallas_call(
        body,
        out_shape=(
            jax.ShapeDtypeStruct((ROWS, owned), BF16),
            jax.ShapeDtypeStruct((2 * HARM, listeners), F32),
        ),
        in_specs=[vmem],
        out_specs=(vmem, vmem),
        compiler_params=pltpu.CompilerParams(vmem_limit_bytes=40 * 2**20),
    )(received)


SUB = 128
KINDS = 3


def pair_sums(lines, weights_ref, points_ref):
    owned = weights_ref.shape[2]
    count = lines.shape[0] // 2
    listeners = lines.shape[1]
    step = min(256, owned)
    scale = TURN * TURN
    over_x = jnp.concatenate([lines[2 * j : 2 * j + 1] for j in range(count)], axis=1)
    over_y = jnp.concatenate([lines[2 * j + 1 : 2 * j + 2] for j in range(count)], axis=1)
    there = scale * (over_x * over_x + over_y * over_y + GROUND * GROUND)
    one, zero = jnp.ones_like(there), jnp.zeros_like(there)
    views = jnp.concatenate(
        thirds((-2.0 * scale) * over_x) + thirds((-2.0 * scale) * over_y) + thirds(there) + [one] * 3 + [zero] * 4,
        axis=0,
    ).astype(BF16)
    width = min(128, count * listeners)
    made = []
    for left in range(0, count * listeners, width):
        view = views[:, left : left + width]
        totals = [[None] * KINDS for _ in range(HARM)]
        pending = []

        def drain(number):
            for _ in range(min(number, len(pending))):
                h, m, begin, pieces = pending.pop(0)
                whole = pieces[0] if len(pieces) == 1 else jnp.concatenate(pieces, axis=0)
                part = weights_ref[h, :, begin : begin + step]
                product = jnp.dot(part, whole, preferred_element_type=F32)
                totals[h][m] = product if totals[h][m] is None else totals[h][m] + product

        for start in range(0, owned, step):
            mats = [[[] for _ in range(KINDS)] for _ in range(HARM)]
            for row in range(start, start + step, SUB):
                square = jnp.dot(points_ref[row : row + SUB, :], view, preferred_element_type=F32)
                inv = lax.rsqrt(square)
                turns = square * inv
                frac = turns - jnp.round(turns)
                half = horner(HALF_SINE, frac * frac) * frac
                versine = half * half
                cosine = 1.0 - versine
                twoc = cosine + cosine
                rest = jnp.maximum(2.0 - versine, 1e-30)
                inv_bf = inv.astype(BF16)
                c_prev, s_prev = inv, None
                c_now = inv * cosine
                s_now = (inv * half) * (rest * lax.rsqrt(rest))
                for h in range(HARM):
                    c_bf, s_bf = c_now.astype(BF16), s_now.astype(BF16)
                    d, e = (inv * c_now).astype(BF16), (inv * s_now).astype(BF16)
                    for m, pair in enumerate(((c_bf, s_bf), (d, e), (inv_bf * d, inv_bf * e))):
                        mats[h][m].append(jnp.concatenate(pair, axis=1))
                    if h < HARM - 1:
                        c_next = twoc * c_now - c_prev
                        s_next = twoc * s_now - s_prev if h else twoc * s_now
                        c_prev, s_prev, c_now, s_now = c_now, s_now, c_next, s_next
                drain(HARM * KINDS * SUB // step)
            drain(HARM * KINDS)
            pending += [(h, m, start, mats[h][m]) for h in range(HARM) for m in range(KINDS)]
        drain(HARM * KINDS)
        ox, oy = over_x[:, left : left + width], over_y[:, left : left + width]
        rows = []
        for h in range(HARM):
            wavenum = WAVENUMBER * (h + 1)
            totals[h] = [half for both in totals[h] for half in (both[:, :width], both[:, width:])]
            cos_sum, sin_sum = totals[h][0], totals[h][1]

            def loads(m):
                t = totals[h][m]
                return [
                    ox * t[2 + c : 3 + c] + oy * t[4 + c : 5 + c] + (t[8 + c : 9 + c] + t[10 + c : 11 + c])
                    for c in (0, 1)
                ]

            (dr, di), (er, ei), (ur, ui), (vr, vi) = loads(2), loads(3), loads(4), loads(5)
            real = wavenum * (er - di) + TURN * (ur + vi)
            imag = wavenum * (ei + dr) + TURN * (ui - vr)
            rows.append(TURN * (wavenum * (sin_sum[0:1] - cos_sum[1:2]) + TURN * real))
            rows.append(TURN * (wavenum * (cos_sum[0:1] + sin_sum[1:2]) + TURN * imag))
        made.append(jnp.concatenate(rows, axis=0))
    return made


def cells_of(lines, weights_ref, points_ref, lanes):
    listeners = lines.shape[1]
    cells = []
    for value in pair_sums(lines, weights_ref, points_ref):
        top = value.astype(BF16).astype(F32)
        split = [top, value - top]
        for j in range(value.shape[1] // listeners):
            cell = [half[:, listeners * j : listeners * j + listeners] for half in split]
            cell.append(jnp.zeros((2 * HARM, lanes - 2 * listeners), F32))
            cells.append(jnp.concatenate(cell, axis=1))
    return cells


def first_kernel(lines_ref, weights_ref, points_ref, cells_ref):
    for j, cell in enumerate(cells_of(lines_ref[...], weights_ref, points_ref, cells_ref.shape[2])):
        cells_ref[j] = cell


def second_kernel(steps, me_ref, lines_ref, weights_ref, points_ref, cells_ref, codes_ref, body_ref, packed_ref):
    nwide, rows, lanes = body_ref.shape
    for o in range(nwide):
        packed_ref[o, :rows, :] = body_ref[o]
    early = cells_ref.shape[0]
    cells = [cells_ref[j] for j in range(early)]
    cells += cells_of(lines_ref[...], weights_ref, points_ref, lanes)
    for j, cell in enumerate(cells):
        owner = me_ref[0] ^ steps[j]
        packed_ref[owner, rows:, :] = (codes_ref[owner] + cell).astype(BF16)


def first_sums(lines, weights, points, lanes):
    owned = weights.shape[2]
    devices = lines.shape[0] // 2
    pairs = devices * lines.shape[1] * owned
    vmem = pl.BlockSpec(memory_space=pltpu.VMEM)
    return pl.pallas_call(
        first_kernel,
        out_shape=jax.ShapeDtypeStruct((devices, 2 * HARM, lanes), F32),
        in_specs=[vmem] * 3,
        out_specs=vmem,
        compiler_params=pltpu.CompilerParams(vmem_limit_bytes=40 * 2**20),
        cost_estimate=pl.CostEstimate(flops=pairs * 2000, bytes_accessed=owned * 70, transcendentals=pairs),
    )(lines, weights, points)


def second_sums(lines, weights, points, cells, codes, body, steps):
    owned = weights.shape[2]
    nwide, rows, lanes = body.shape
    pairs = lines.shape[0] // 2 * lines.shape[1] * owned
    vmem = pl.BlockSpec(memory_space=pltpu.VMEM)
    me = lax.axis_index("wide").reshape(1)

    def kernel(*refs):
        second_kernel(steps, *refs)

    return pl.pallas_call(
        kernel,
        out_shape=jax.ShapeDtypeStruct((nwide, rows + 8, lanes), BF16),
        in_specs=[pl.BlockSpec(memory_space=pltpu.SMEM)] + [vmem] * 6,
        out_specs=vmem,
        compiler_params=pltpu.CompilerParams(vmem_limit_bytes=40 * 2**20),
        cost_estimate=pl.CostEstimate(flops=pairs * 2000, bytes_accessed=owned * 70, transcendentals=pairs),
    )(me, lines, weights, points, cells, codes, body)


def swap(x, nwide, bit):
    return lax.ppermute(x, "wide", [(i, i ^ bit) for i in range(nwide)])


def shards(flow, positions, normals, panel_ids, observers):
    owned = flow.shape[2]
    nwide = lax.axis_size("wide")
    listeners = observers.shape[1]
    near = nwide // 4
    others = [swap(observers, nwide, n) for n in range(1, near)]
    spectra, weights, points, ids, mine = sources(flow, normals, positions, panel_ids, observers)
    others, spectra = lax.optimization_barrier((others, spectra))
    lines = jnp.concatenate([mine] + others, axis=0)
    other = swap(lines, nwide, near)
    packed, codes = pack(spectra, ids, nwide)
    other, packed = lax.optimization_barrier((other, packed))
    lines = jnp.concatenate([lines, other], axis=0)
    other = swap(lines, nwide, 2 * near)
    cells = first_sums(lines, weights, points, packed.shape[2])
    other, cells = lax.optimization_barrier((other, cells))
    steps = [n ^ z for z in range(0, 4 * near, near) for n in range(near)]
    packed = second_sums(other, weights, points, cells, codes, packed, steps)
    received = lax.all_to_all(packed, "wide", split_axis=0, concat_axis=0, tiled=True)
    panel_spectra, pressure = place(received, owned, listeners)
    return (panel_spectra, pressure.T)


def solution(mesh):
    placed = (
        P(None, None, ("case", "wide")),
        P(None, ("case", "wide")),
        P(None, ("case", "wide")),
        P(("case", "wide")),
        P(None, ("case", "wide")),
    )
    return jax.shard_map(
        shards,
        mesh=mesh,
        in_specs=placed,
        out_specs=(P(None, ("case", "wide")), P(("case", "wide"), None)),
        check_vma=False,
    )
```

```python
import math

import jax
import jax.numpy as jnp
import numpy as np
from jax import lax
from jax.experimental import pallas as pl
from jax.experimental.pallas import tpu as pltpu
from jax.sharding import PartitionSpec as P

NT = 16
HARM = 4
ROWS = 8 * HARM
WAVENUMBER = 2.0
GROUND = 3.0
LOW = 256
F32 = jnp.float32
BF16 = jnp.bfloat16
NT_DIMS = (((1,), (1,)), ((), ()))


def fit(function, degree):
    nodes = np.cos(np.pi * (np.arange(64) + 0.5) / 64) * 0.5
    squares = nodes * nodes
    powers = np.stack([squares**d for d in range(degree + 1)], axis=1)
    return [float(c) for c in np.linalg.lstsq(powers, function(nodes), rcond=None)[0]]


TURN = WAVENUMBER / (2.0 * math.pi)
HALF_SINE = fit(lambda f: math.sqrt(2.0) * np.sin(np.pi * f) / f, 4)


def horner(coefficients, x):
    value = coefficients[-1]
    for c in coefficients[-2::-1]:
        value = value * x + c
    return value


def thirds(x):
    first = x.astype(BF16).astype(F32)
    second = (x - first).astype(BF16).astype(F32)
    return [first, second, x - first - second]


def dft_split():
    samples = np.arange(NT)[:, None]
    harmonic = np.arange(1, HARM + 1)[None, :]
    angle = 2.0 * np.pi / NT * samples * harmonic
    table = np.stack([np.cos(angle), -np.sin(angle)], axis=2) * (2.0 / NT)
    table = table.reshape(NT, 2 * HARM).T
    block = np.kron(np.eye(4), table).astype(np.float32)
    order = [8 * a + 2 * h + c for h in range(HARM) for a in range(4) for c in range(2)]
    block = np.concatenate([block, block[order]], axis=0)
    high = block.astype(jnp.bfloat16)
    low = (block - high.astype(np.float32)).astype(jnp.bfloat16)
    return np.concatenate([high, high, low, low], axis=1)


def pack_shape(nwide, owned):
    capacity = 2 * owned // nwide
    lanes = min(capacity, 128)
    subs = capacity // lanes
    return capacity, lanes, subs, ROWS * subs + 8


def source_kernel(
    flow_hbm, normals_hbm, place_hbm, table_hbm, ids_hbm, over_hbm,
    spectra_ref, weights_ref, points_ref, ids_ref, mine_ref,
    flow_ref, normals_ref, place_ref, table_ref, sems,
):
    owned = flow_ref.shape[2]
    step = min(256, owned)
    copies = [
        pltpu.make_async_copy(normals_hbm, normals_ref, sems.at[0]),
        pltpu.make_async_copy(place_hbm, place_ref, sems.at[1]),
        pltpu.make_async_copy(table_hbm, table_ref, sems.at[2]),
        pltpu.make_async_copy(flow_hbm, flow_ref, sems.at[5]),
    ]
    passed = [
        pltpu.make_async_copy(ids_hbm, ids_ref, sems.at[3]),
        pltpu.make_async_copy(over_hbm, mine_ref, sems.at[4]),
    ]
    for copy in copies + passed:
        copy.start()
    for copy in copies:
        copy.wait()
    table = table_ref[...]
    scale = TURN * TURN
    for start in range(0, owned, step):
        cols = slice(start, start + step)
        normal = normals_ref[:, cols].astype(F32)
        n0, n1, n2 = normal[0:1], normal[1:2], normal[2:3]
        density = 1.0 + 0.2 * flow_ref[0, :, cols].astype(F32)
        v0 = 0.5 * flow_ref[1, :, cols].astype(F32)
        v1 = 0.5 * flow_ref[2, :, cols].astype(F32)
        v2 = 0.5 * flow_ref[3, :, cols].astype(F32)
        fluct = flow_ref[4, :, cols].astype(F32)
        across = v0 * n0 + v1 * n1 + v2 * n2
        source = density * across
        parts = jnp.concatenate(
            [source, fluct * n0 + v0 * source, fluct * n1 + v1 * source, fluct * n2 + v2 * source], axis=0
        )
        top = parts.astype(BF16)
        rest = (parts - top.astype(F32)).astype(BF16)
        both = jnp.concatenate([top, rest, top, rest], axis=0)
        spectra = jnp.dot(table, both, preferred_element_type=F32).astype(BF16)
        spectra_ref[:, cols] = spectra[:ROWS]
        by_harmonic = spectra[ROWS:].astype(F32)
        place = place_ref[:, cols].astype(F32)
        px, py, pz = place[0:1], place[1:2], place[2:3]
        down = pz + GROUND
        none = jnp.zeros_like(px)
        factors = jnp.concatenate([none, none, px, px, py, py, down, down], axis=0)
        for h in range(HARM):
            group = by_harmonic[8 * h : 8 * h + 8]
            shares = group * factors
            along = -(shares[2:4] + shares[4:6] + shares[6:8])
            along_high = along.astype(BF16).astype(F32)
            weights_ref[h, :, cols] = jnp.concatenate(
                [group, along_high, along - along_high, jnp.zeros((4, step), F32)], axis=0
            ).astype(BF16)
        here = scale * (px * px + py * py + pz * pz + (2.0 * GROUND) * pz)
        one = jnp.ones_like(here)
        points = jnp.concatenate([px] * 3 + [py] * 3 + [one] * 3 + thirds(here) + [none] * 4, axis=0)
        points_ref[cols, :] = points.T.astype(BF16)
    for copy in passed:
        copy.wait()


def sources(flow, normals, positions, ids, observers):
    owned = flow.shape[2]
    vmem = pl.BlockSpec(memory_space=pltpu.VMEM)
    anywhere = pl.BlockSpec(memory_space=pl.ANY)
    table = jnp.asarray(dft_split())
    arrays = (flow, normals, positions, table, ids.reshape(1, owned), observers)
    return pl.pallas_call(
        source_kernel,
        out_shape=(
            jax.ShapeDtypeStruct((ROWS, owned), BF16),
            jax.ShapeDtypeStruct((HARM, 16, owned), BF16),
            jax.ShapeDtypeStruct((owned, 16), BF16),
            jax.ShapeDtypeStruct((1, owned), jnp.int32),
            jax.ShapeDtypeStruct(observers.shape, F32),
        ),
        in_specs=[anywhere] * 6,
        out_specs=(vmem,) * 5,
        scratch_shapes=[
            pltpu.VMEM(flow.shape, BF16),
            pltpu.VMEM(normals.shape, BF16),
            pltpu.VMEM(positions.shape, BF16),
            pltpu.VMEM(table.shape, BF16),
            pltpu.SemaphoreType.DMA((6,)),
        ],
        compiler_params=pltpu.CompilerParams(vmem_limit_bytes=32 * 2**20),
    )(*(pltpu.with_memory_space_constraint(x, pltpu.HBM) for x in arrays))


def pack_kernel(nwide, spectra_ref, ids_ref, packed_ref, codes_ref, left, right):
    owned = spectra_ref.shape[1]
    capacity, lanes, subs, _ = pack_shape(nwide, owned)
    step = min(256, owned)
    upper = (
        lax.broadcasted_iota(jnp.int32, (step, step), 0)
        < lax.broadcasted_iota(jnp.int32, (step, step), 1)
    ).astype(F32).astype(BF16)
    ids = ids_ref[...]
    owner = ids // owned
    local = ids - owner * owned
    high = local // LOW
    code_high = (high + 1).astype(F32)
    code_low = (local - high * LOW).astype(F32)
    carry = jnp.zeros((nwide, 1), F32)
    which = lax.broadcasted_iota(jnp.int32, (nwide, step), 0)
    slots = lax.broadcasted_iota(jnp.int32, (capacity, step), 0).astype(F32)
    codes_row = lax.broadcasted_iota(jnp.int32, (8, step), 0)
    for start in range(0, owned, step):
        cols = slice(start, start + step)
        own = which == owner[:, cols]
        ownf = own.astype(F32)
        before = jnp.dot(ownf.astype(BF16), upper, preferred_element_type=F32) + carry
        rank = jnp.sum(before * ownf, axis=0, keepdims=True)
        carry = before[:, step - 1 : step] + ownf[:, step - 1 : step]
        right[:, cols] = (slots == rank).astype(F32).astype(BF16)
        codes = jnp.where(codes_row == 0, code_high[:, cols], jnp.where(codes_row == 1, code_low[:, cols], 0.0))
        codes = jnp.concatenate([codes, jnp.zeros_like(codes)], axis=0).astype(BF16)
        values = jnp.concatenate([spectra_ref[:, cols], codes], axis=0)
        for o in range(nwide):
            left[48 * o : 48 * o + 48, cols] = jnp.where(owner[:, cols] == o, values, jnp.zeros_like(values))
    packed = lax.dot_general(left[...], right[...], NT_DIMS, preferred_element_type=F32)
    lane = lax.broadcasted_iota(jnp.int32, (8, lanes), 1)
    for o in range(nwide):
        block = packed[48 * o : 48 * o + 48]
        for s in range(subs):
            packed_ref[o, ROWS * s : ROWS * s + ROWS, :] = block[:ROWS, lanes * s : lanes * s + lanes].astype(BF16)
        codes = []
        for s in range(subs):
            upper_half = block[ROWS : ROWS + 8, lanes * s : lanes * s + lanes]
            lower_half = jnp.concatenate([upper_half[:, lanes // 2 :], upper_half[:, : lanes // 2]], axis=1)
            codes += [lower_half[:2], upper_half[:2]]
        codes = jnp.concatenate(codes + [jnp.zeros((8 - 4 * subs, lanes), F32)] * (subs == 1), axis=0)
        codes_ref[o] = jnp.where(lane < lanes // 2, 0.0, codes)


def pack(spectra, ids, nwide):
    owned = spectra.shape[1]
    capacity, lanes, subs, _ = pack_shape(nwide, owned)
    vmem = pl.BlockSpec(memory_space=pltpu.VMEM)

    def body(*refs):
        pack_kernel(nwide, *refs)

    return pl.pallas_call(
        body,
        out_shape=(
            jax.ShapeDtypeStruct((nwide, ROWS * subs, lanes), BF16),
            jax.ShapeDtypeStruct((nwide, 8, lanes), F32),
        ),
        in_specs=[vmem] * 2,
        out_specs=(vmem, vmem),
        scratch_shapes=[
            pltpu.VMEM((48 * nwide, owned), BF16),
            pltpu.VMEM((capacity, owned), BF16),
        ],
        compiler_params=pltpu.CompilerParams(vmem_limit_bytes=40 * 2**20),
    )(spectra, ids)


def place_kernel(scale, received_ref, spectra_ref, pressure_ref):
    nwide, depth, lanes = received_ref.shape
    owned = spectra_ref.shape[1]
    listeners = pressure_ref.shape[1]
    subs = (depth - 8) // ROWS
    heights = owned // LOW
    group = max(1, 256 // (lanes * subs))
    width = lanes * subs * group
    lows = lax.broadcasted_iota(jnp.int32, (LOW, width), 0).astype(F32)
    total = jnp.zeros((heights * ROWS, LOW), F32)
    sums = jnp.zeros((2 * HARM, lanes), F32)
    lower = lax.broadcasted_iota(jnp.int32, (1, lanes), 1) < lanes // 2
    for first in range(0, nwide, group):
        blocks, high, low = [], [], []
        for o in range(first, first + group):
            codes = received_ref[o, ROWS * subs : ROWS * subs + 8, :].astype(F32)
            sums = sums + codes
            turned = jnp.concatenate([codes[:, lanes // 2 :], codes[:, : lanes // 2]], axis=1)
            for s in range(subs):
                blocks.append(received_ref[o, ROWS * s : ROWS * s + ROWS, :])
                high.append(jnp.where(lower, turned[4 * s : 4 * s + 1], codes[4 * s + 2 : 4 * s + 3]))
                low.append(jnp.where(lower, turned[4 * s + 1 : 4 * s + 2], codes[4 * s + 3 : 4 * s + 4]))
        values = jnp.concatenate(blocks, axis=1)
        high = jnp.concatenate(high, axis=1)
        low = jnp.concatenate(low, axis=1)
        spread = (lows == low).astype(F32).astype(BF16)
        picked = jnp.concatenate(
            [jnp.where(high == h + 1.0, values, jnp.zeros_like(values)) for h in range(heights)], axis=0
        )
        total = total + lax.dot_general(picked, spread, NT_DIMS, preferred_element_type=F32)
    for h in range(heights):
        spectra_ref[:, LOW * h : LOW * h + LOW] = total[ROWS * h : ROWS * h + ROWS].astype(BF16)
    pressure_ref[...] = scale * (sums[:, listeners : 2 * listeners] + sums[:, :listeners])


def place(received, owned, listeners):
    nwide = received.shape[0]
    vmem = pl.BlockSpec(memory_space=pltpu.VMEM)
    scale = 2.0 / math.sqrt(owned * nwide)

    def body(*refs):
        place_kernel(scale, *refs)

    return pl.pallas_call(
        body,
        out_shape=(
            jax.ShapeDtypeStruct((ROWS, owned), BF16),
            jax.ShapeDtypeStruct((2 * HARM, listeners), F32),
        ),
        in_specs=[vmem],
        out_specs=(vmem, vmem),
        compiler_params=pltpu.CompilerParams(vmem_limit_bytes=40 * 2**20),
    )(received)


SUB = 128
KINDS = 3


def pair_sums(lines, weights_ref, points_ref):
    owned = weights_ref.shape[2]
    count = lines.shape[0] // 2
    listeners = lines.shape[1]
    step = min(256, owned)
    scale = TURN * TURN
    over_x = jnp.concatenate([lines[2 * j : 2 * j + 1] for j in range(count)], axis=1)
    over_y = jnp.concatenate([lines[2 * j + 1 : 2 * j + 2] for j in range(count)], axis=1)
    there = scale * (over_x * over_x + over_y * over_y + GROUND * GROUND)
    one, zero = jnp.ones_like(there), jnp.zeros_like(there)
    views = jnp.concatenate(
        thirds((-2.0 * scale) * over_x) + thirds((-2.0 * scale) * over_y) + thirds(there) + [one] * 3 + [zero] * 4,
        axis=0,
    ).astype(BF16)
    width = min(128, count * listeners)
    made = []
    for left in range(0, count * listeners, width):
        view = views[:, left : left + width]
        totals = [[None] * KINDS for _ in range(HARM)]
        pending = []

        def drain(number):
            for _ in range(min(number, len(pending))):
                h, m, begin, pieces = pending.pop(0)
                whole = pieces[0] if len(pieces) == 1 else jnp.concatenate(pieces, axis=0)
                part = weights_ref[h, :, begin : begin + step]
                product = jnp.dot(part, whole, preferred_element_type=F32)
                totals[h][m] = product if totals[h][m] is None else totals[h][m] + product

        for start in range(0, owned, step):
            mats = [[[] for _ in range(KINDS)] for _ in range(HARM)]
            for row in range(start, start + step, SUB):
                square = jnp.dot(points_ref[row : row + SUB, :], view, preferred_element_type=F32)
                inv = lax.rsqrt(square)
                turns = square * inv
                frac = turns - jnp.round(turns)
                half = horner(HALF_SINE, frac * frac) * frac
                versine = half * half
                cosine = 1.0 - versine
                twoc = cosine + cosine
                rest = jnp.maximum(2.0 - versine, 1e-30)
                inv_bf = inv.astype(BF16)
                c_prev, s_prev = inv, None
                c_now = inv * cosine
                s_now = (inv * half) * (rest * lax.rsqrt(rest))
                for h in range(HARM):
                    c_bf, s_bf = c_now.astype(BF16), s_now.astype(BF16)
                    d, e = (inv * c_now).astype(BF16), (inv * s_now).astype(BF16)
                    for m, pair in enumerate(((c_bf, s_bf), (d, e), (inv_bf * d, inv_bf * e))):
                        mats[h][m].append(jnp.concatenate(pair, axis=1))
                    if h < HARM - 1:
                        c_next = twoc * c_now - c_prev
                        s_next = twoc * s_now - s_prev if h else twoc * s_now
                        c_prev, s_prev, c_now, s_now = c_now, s_now, c_next, s_next
                drain(HARM * KINDS * SUB // step)
            drain(HARM * KINDS)
            pending += [(h, m, start, mats[h][m]) for h in range(HARM) for m in range(KINDS)]
        drain(HARM * KINDS)
        ox, oy = over_x[:, left : left + width], over_y[:, left : left + width]
        rows = []
        for h in range(HARM):
            wavenum = WAVENUMBER * (h + 1)
            totals[h] = [half for both in totals[h] for half in (both[:, :width], both[:, width:])]
            cos_sum, sin_sum, d, e, u, v = totals[h]

            def loads(t):
                return ox * t[2:4] + oy * t[4:6] + (t[8:10] + t[10:12])

            plain = wavenum * sin_sum[:2] + loads((wavenum * TURN) * e + (TURN * TURN) * u)
            turned = wavenum * cos_sum[:2] + loads((wavenum * TURN) * d - (TURN * TURN) * v)
            rows.append(TURN * (plain + jnp.concatenate([-turned[1:2], turned[0:1]], axis=0)))
        made.append(jnp.concatenate(rows, axis=0))
    return made


def cells_of(lines, weights_ref, points_ref, lanes):
    listeners = lines.shape[1]
    cells = []
    for value in pair_sums(lines, weights_ref, points_ref):
        top = value.astype(BF16).astype(F32)
        split = [top, value - top]
        for j in range(value.shape[1] // listeners):
            cell = [half[:, listeners * j : listeners * j + listeners] for half in split]
            cell.append(jnp.zeros((2 * HARM, lanes - 2 * listeners), F32))
            cells.append(jnp.concatenate(cell, axis=1))
    return cells


def first_kernel(lines_ref, weights_ref, points_ref, cells_ref):
    for j, cell in enumerate(cells_of(lines_ref[...], weights_ref, points_ref, cells_ref.shape[2])):
        cells_ref[j] = cell


def second_kernel(steps, me_ref, lines_ref, weights_ref, points_ref, cells_ref, codes_ref, body_ref, packed_ref):
    nwide, rows, lanes = body_ref.shape
    for o in range(nwide):
        packed_ref[o, :rows, :] = body_ref[o]
    early = cells_ref.shape[0]
    cells = [cells_ref[j] for j in range(early)]
    cells += cells_of(lines_ref[...], weights_ref, points_ref, lanes)
    for j, cell in enumerate(cells):
        owner = me_ref[0] ^ steps[j]
        packed_ref[owner, rows:, :] = (codes_ref[owner] + cell).astype(BF16)


def first_sums(lines, weights, points, lanes):
    owned = weights.shape[2]
    devices = lines.shape[0] // 2
    pairs = devices * lines.shape[1] * owned
    vmem = pl.BlockSpec(memory_space=pltpu.VMEM)
    return pl.pallas_call(
        first_kernel,
        out_shape=jax.ShapeDtypeStruct((devices, 2 * HARM, lanes), F32),
        in_specs=[vmem] * 3,
        out_specs=vmem,
        compiler_params=pltpu.CompilerParams(vmem_limit_bytes=40 * 2**20),
        cost_estimate=pl.CostEstimate(flops=pairs * 2000, bytes_accessed=owned * 70, transcendentals=pairs),
    )(lines, weights, points)


def second_sums(lines, weights, points, cells, codes, body, steps):
    owned = weights.shape[2]
    nwide, rows, lanes = body.shape
    pairs = lines.shape[0] // 2 * lines.shape[1] * owned
    vmem = pl.BlockSpec(memory_space=pltpu.VMEM)
    me = lax.axis_index("wide").reshape(1)

    def kernel(*refs):
        second_kernel(steps, *refs)

    return pl.pallas_call(
        kernel,
        out_shape=jax.ShapeDtypeStruct((nwide, rows + 8, lanes), BF16),
        in_specs=[pl.BlockSpec(memory_space=pltpu.SMEM)] + [vmem] * 6,
        out_specs=vmem,
        compiler_params=pltpu.CompilerParams(vmem_limit_bytes=40 * 2**20),
        cost_estimate=pl.CostEstimate(flops=pairs * 2000, bytes_accessed=owned * 70, transcendentals=pairs),
    )(me, lines, weights, points, cells, codes, body)


def swap(x, nwide, bit):
    return lax.ppermute(x, "wide", [(i, i ^ bit) for i in range(nwide)])


def shards(flow, positions, normals, panel_ids, observers):
    owned = flow.shape[2]
    nwide = lax.axis_size("wide")
    listeners = observers.shape[1]
    near = nwide // 4
    others = [swap(observers, nwide, n) for n in range(1, near)]
    spectra, weights, points, ids, mine = sources(flow, normals, positions, panel_ids, observers)
    others, spectra = lax.optimization_barrier((others, spectra))
    lines = jnp.concatenate([mine] + others, axis=0)
    other = swap(lines, nwide, near)
    packed, codes = pack(spectra, ids, nwide)
    other, packed = lax.optimization_barrier((other, packed))
    lines = jnp.concatenate([lines, other], axis=0)
    other = swap(lines, nwide, 2 * near)
    cells = first_sums(lines, weights, points, packed.shape[2])
    other, cells = lax.optimization_barrier((other, cells))
    steps = [n ^ z for z in range(0, 4 * near, near) for n in range(near)]
    packed = second_sums(other, weights, points, cells, codes, packed, steps)
    received = lax.all_to_all(packed, "wide", split_axis=0, concat_axis=0, tiled=True)
    panel_spectra, pressure = place(received, owned, listeners)
    return (panel_spectra, pressure.T)


def solution(mesh):
    placed = (
        P(None, None, ("case", "wide")),
        P(None, ("case", "wide")),
        P(None, ("case", "wide")),
        P(("case", "wide")),
        P(None, ("case", "wide")),
    )
    return jax.shard_map(
        shards,
        mesh=mesh,
        in_specs=placed,
        out_specs=(P(None, ("case", "wide")), P(("case", "wide"), None)),
        check_vma=False,
    )
```

```python
import math

import jax
import jax.numpy as jnp
import numpy as np
from jax import lax
from jax.experimental import pallas as pl
from jax.experimental.pallas import tpu as pltpu
from jax.sharding import PartitionSpec as P

NT = 16
HARM = 4
ROWS = 8 * HARM
WAVENUMBER = 2.0
GROUND = 3.0
LOW = 256
F32 = jnp.float32
BF16 = jnp.bfloat16
NT_DIMS = (((1,), (1,)), ((), ()))


def fit(function, degree):
    nodes = np.cos(np.pi * (np.arange(64) + 0.5) / 64) * 0.5
    squares = nodes * nodes
    powers = np.stack([squares**d for d in range(degree + 1)], axis=1)
    return [float(c) for c in np.linalg.lstsq(powers, function(nodes), rcond=None)[0]]


TURN = WAVENUMBER / (2.0 * math.pi)
HALF_SINE = fit(lambda f: math.sqrt(2.0) * np.sin(np.pi * f) / f, 4)


def horner(coefficients, x):
    value = coefficients[-1]
    for c in coefficients[-2::-1]:
        value = value * x + c
    return value


def thirds(x):
    first = x.astype(BF16).astype(F32)
    second = (x - first).astype(BF16).astype(F32)
    return [first, second, x - first - second]


def dft_split():
    samples = np.arange(NT)[:, None]
    harmonic = np.arange(1, HARM + 1)[None, :]
    angle = 2.0 * np.pi / NT * samples * harmonic
    table = np.stack([np.cos(angle), -np.sin(angle)], axis=2) * (2.0 / NT)
    table = table.reshape(NT, 2 * HARM).T
    block = np.kron(np.eye(4), table).astype(np.float32)
    order = [8 * a + 2 * h + c for h in range(HARM) for a in range(4) for c in range(2)]
    block = np.concatenate([block, block[order]], axis=0)
    high = block.astype(jnp.bfloat16)
    low = (block - high.astype(np.float32)).astype(jnp.bfloat16)
    return np.concatenate([high, high, low, low], axis=1)


def pack_shape(nwide, owned):
    capacity = 2 * owned // nwide
    lanes = min(capacity, 128)
    subs = capacity // lanes
    return capacity, lanes, subs, ROWS * subs + 8


def source_kernel(
    flow_hbm, normals_hbm, place_hbm, table_hbm, ids_hbm, over_hbm,
    spectra_ref, weights_ref, points_ref, ids_ref, mine_ref,
    flow_ref, normals_ref, place_ref, table_ref, sems,
):
    owned = flow_ref.shape[2]
    step = min(256, owned)
    copies = [
        pltpu.make_async_copy(normals_hbm, normals_ref, sems.at[0]),
        pltpu.make_async_copy(place_hbm, place_ref, sems.at[1]),
        pltpu.make_async_copy(table_hbm, table_ref, sems.at[2]),
        pltpu.make_async_copy(flow_hbm, flow_ref, sems.at[5]),
    ]
    passed = [
        pltpu.make_async_copy(ids_hbm, ids_ref, sems.at[3]),
        pltpu.make_async_copy(over_hbm, mine_ref, sems.at[4]),
    ]
    for copy in copies + passed:
        copy.start()
    for copy in copies:
        copy.wait()
    table = table_ref[...]
    scale = TURN * TURN
    for start in range(0, owned, step):
        cols = slice(start, start + step)
        normal = normals_ref[:, cols].astype(F32)
        n0, n1, n2 = normal[0:1], normal[1:2], normal[2:3]
        density = 1.0 + 0.2 * flow_ref[0, :, cols].astype(F32)
        v0 = 0.5 * flow_ref[1, :, cols].astype(F32)
        v1 = 0.5 * flow_ref[2, :, cols].astype(F32)
        v2 = 0.5 * flow_ref[3, :, cols].astype(F32)
        fluct = flow_ref[4, :, cols].astype(F32)
        across = v0 * n0 + v1 * n1 + v2 * n2
        source = density * across
        parts = jnp.concatenate(
            [source, fluct * n0 + v0 * source, fluct * n1 + v1 * source, fluct * n2 + v2 * source], axis=0
        )
        top = parts.astype(BF16)
        rest = (parts - top.astype(F32)).astype(BF16)
        both = jnp.concatenate([top, rest, top, rest], axis=0)
        spectra = jnp.dot(table, both, preferred_element_type=F32).astype(BF16)
        spectra_ref[:, cols] = spectra[:ROWS]
        by_harmonic = spectra[ROWS:].astype(F32)
        place = place_ref[:, cols].astype(F32)
        px, py, pz = place[0:1], place[1:2], place[2:3]
        down = pz + GROUND
        none = jnp.zeros_like(px)
        factors = jnp.concatenate([none, none, px, px, py, py, down, down], axis=0)
        for h in range(HARM):
            group = by_harmonic[8 * h : 8 * h + 8]
            shares = group * factors
            along = -(shares[2:4] + shares[4:6] + shares[6:8])
            along_high = along.astype(BF16).astype(F32)
            weights_ref[h, :, cols] = jnp.concatenate(
                [group, along_high, along - along_high, jnp.zeros((4, step), F32)], axis=0
            ).astype(BF16)
        here = scale * (px * px + py * py + pz * pz + (2.0 * GROUND) * pz)
        one = jnp.ones_like(here)
        points = jnp.concatenate([px] * 3 + [py] * 3 + [one] * 3 + thirds(here) + [none] * 4, axis=0)
        points_ref[cols, :] = points.T.astype(BF16)
    for copy in passed:
        copy.wait()


def sources(flow, normals, positions, ids, observers):
    owned = flow.shape[2]
    vmem = pl.BlockSpec(memory_space=pltpu.VMEM)
    anywhere = pl.BlockSpec(memory_space=pl.ANY)
    table = jnp.asarray(dft_split())
    arrays = (flow, normals, positions, table, ids.reshape(1, owned), observers)
    return pl.pallas_call(
        source_kernel,
        out_shape=(
            jax.ShapeDtypeStruct((ROWS, owned), BF16),
            jax.ShapeDtypeStruct((HARM, 16, owned), BF16),
            jax.ShapeDtypeStruct((owned, 16), BF16),
            jax.ShapeDtypeStruct((1, owned), jnp.int32),
            jax.ShapeDtypeStruct(observers.shape, F32),
        ),
        in_specs=[anywhere] * 6,
        out_specs=(vmem,) * 5,
        scratch_shapes=[
            pltpu.VMEM(flow.shape, BF16),
            pltpu.VMEM(normals.shape, BF16),
            pltpu.VMEM(positions.shape, BF16),
            pltpu.VMEM(table.shape, BF16),
            pltpu.SemaphoreType.DMA((6,)),
        ],
        compiler_params=pltpu.CompilerParams(vmem_limit_bytes=32 * 2**20),
    )(*(pltpu.with_memory_space_constraint(x, pltpu.HBM) for x in arrays))


def pack_kernel(nwide, spectra_ref, ids_ref, packed_ref, codes_ref, left, right):
    owned = spectra_ref.shape[1]
    capacity, lanes, subs, _ = pack_shape(nwide, owned)
    step = min(256, owned)
    upper = (
        lax.broadcasted_iota(jnp.int32, (step, step), 0)
        < lax.broadcasted_iota(jnp.int32, (step, step), 1)
    ).astype(F32).astype(BF16)
    ids = ids_ref[...]
    owner = ids // owned
    local = ids - owner * owned
    high = local // LOW
    code_high = (high + 1).astype(F32)
    code_low = (local - high * LOW).astype(F32)
    carry = jnp.zeros((nwide, 1), F32)
    which = lax.broadcasted_iota(jnp.int32, (nwide, step), 0)
    slots = lax.broadcasted_iota(jnp.int32, (capacity, step), 0).astype(F32)
    codes_row = lax.broadcasted_iota(jnp.int32, (8, step), 0)
    for start in range(0, owned, step):
        cols = slice(start, start + step)
        own = which == owner[:, cols]
        ownf = own.astype(F32)
        before = jnp.dot(ownf.astype(BF16), upper, preferred_element_type=F32) + carry
        rank = jnp.sum(before * ownf, axis=0, keepdims=True)
        carry = before[:, step - 1 : step] + ownf[:, step - 1 : step]
        right[:, cols] = (slots == rank).astype(F32).astype(BF16)
        codes = jnp.where(codes_row == 0, code_high[:, cols], jnp.where(codes_row == 1, code_low[:, cols], 0.0))
        codes = jnp.concatenate([codes, jnp.zeros_like(codes)], axis=0).astype(BF16)
        values = jnp.concatenate([spectra_ref[:, cols], codes], axis=0)
        for o in range(nwide):
            left[48 * o : 48 * o + 48, cols] = jnp.where(owner[:, cols] == o, values, jnp.zeros_like(values))
    packed = lax.dot_general(left[...], right[...], NT_DIMS, preferred_element_type=F32)
    lane = lax.broadcasted_iota(jnp.int32, (8, lanes), 1)
    for o in range(nwide):
        block = packed[48 * o : 48 * o + 48]
        for s in range(subs):
            packed_ref[o, ROWS * s : ROWS * s + ROWS, :] = block[:ROWS, lanes * s : lanes * s + lanes].astype(BF16)
        codes = []
        for s in range(subs):
            upper_half = block[ROWS : ROWS + 8, lanes * s : lanes * s + lanes]
            lower_half = jnp.concatenate([upper_half[:, lanes // 2 :], upper_half[:, : lanes // 2]], axis=1)
            codes += [lower_half[:2], upper_half[:2]]
        codes = jnp.concatenate(codes + [jnp.zeros((8 - 4 * subs, lanes), F32)] * (subs == 1), axis=0)
        codes_ref[o] = jnp.where(lane < lanes // 2, 0.0, codes)


def pack(spectra, ids, nwide):
    owned = spectra.shape[1]
    capacity, lanes, subs, _ = pack_shape(nwide, owned)
    vmem = pl.BlockSpec(memory_space=pltpu.VMEM)

    def body(*refs):
        pack_kernel(nwide, *refs)

    return pl.pallas_call(
        body,
        out_shape=(
            jax.ShapeDtypeStruct((nwide, ROWS * subs, lanes), BF16),
            jax.ShapeDtypeStruct((nwide, 8, lanes), F32),
        ),
        in_specs=[vmem] * 2,
        out_specs=(vmem, vmem),
        scratch_shapes=[
            pltpu.VMEM((48 * nwide, owned), BF16),
            pltpu.VMEM((capacity, owned), BF16),
        ],
        compiler_params=pltpu.CompilerParams(vmem_limit_bytes=40 * 2**20),
    )(spectra, ids)


def place_kernel(scale, received_ref, spectra_ref, pressure_ref):
    nwide, depth, lanes = received_ref.shape
    owned = spectra_ref.shape[1]
    listeners = pressure_ref.shape[1]
    subs = (depth - 8) // ROWS
    heights = owned // LOW
    group = max(1, 256 // (lanes * subs))
    width = lanes * subs * group
    lows = lax.broadcasted_iota(jnp.int32, (LOW, width), 0).astype(F32)
    all_picked, all_spread = [], []
    sums = jnp.zeros((2 * HARM, lanes), F32)
    lower = lax.broadcasted_iota(jnp.int32, (1, lanes), 1) < lanes // 2
    for first in range(0, nwide, group):
        blocks, high, low = [], [], []
        for o in range(first, first + group):
            codes = received_ref[o, ROWS * subs : ROWS * subs + 8, :].astype(F32)
            sums = sums + codes
            turned = jnp.concatenate([codes[:, lanes // 2 :], codes[:, : lanes // 2]], axis=1)
            for s in range(subs):
                blocks.append(received_ref[o, ROWS * s : ROWS * s + ROWS, :])
                high.append(jnp.where(lower, turned[4 * s : 4 * s + 1], codes[4 * s + 2 : 4 * s + 3]))
                low.append(jnp.where(lower, turned[4 * s + 1 : 4 * s + 2], codes[4 * s + 3 : 4 * s + 4]))
        values = jnp.concatenate(blocks, axis=1)
        high = jnp.concatenate(high, axis=1)
        low = jnp.concatenate(low, axis=1)
        spread = (lows == low).astype(F32).astype(BF16)
        masks = (lax.broadcasted_iota(jnp.int32, (heights, width), 0).astype(F32) + 1.0 == high).astype(F32)
        picked = []
        for h in range(heights):
            mask = jnp.broadcast_to(masks[h : h + 1], (16, width)).astype(BF16)
            picked += [values[16 * p : 16 * p + 16] * mask for p in range(ROWS // 16)]
        picked = jnp.concatenate(picked, axis=0)
        all_picked.append(picked)
        all_spread.append(spread)
    total = lax.dot_general(
        jnp.concatenate(all_picked, axis=1), jnp.concatenate(all_spread, axis=1), NT_DIMS, preferred_element_type=F32
    )
    for h in range(heights):
        spectra_ref[:, LOW * h : LOW * h + LOW] = total[ROWS * h : ROWS * h + ROWS].astype(BF16)
    pressure_ref[...] = scale * (sums[:, listeners : 2 * listeners] + sums[:, :listeners])


def place(received, owned, listeners):
    nwide = received.shape[0]
    vmem = pl.BlockSpec(memory_space=pltpu.VMEM)
    scale = 2.0 / math.sqrt(owned * nwide)

    def body(*refs):
        place_kernel(scale, *refs)

    return pl.pallas_call(
        body,
        out_shape=(
            jax.ShapeDtypeStruct((ROWS, owned), BF16),
            jax.ShapeDtypeStruct((2 * HARM, listeners), F32),
        ),
        in_specs=[vmem],
        out_specs=(vmem, vmem),
        compiler_params=pltpu.CompilerParams(vmem_limit_bytes=40 * 2**20),
    )(received)


SUB = 128
KINDS = 3


def pair_sums(lines, weights_ref, points_ref):
    owned = weights_ref.shape[2]
    count = lines.shape[0] // 2
    listeners = lines.shape[1]
    step = min(256, owned)
    scale = TURN * TURN
    over_x = jnp.concatenate([lines[2 * j : 2 * j + 1] for j in range(count)], axis=1)
    over_y = jnp.concatenate([lines[2 * j + 1 : 2 * j + 2] for j in range(count)], axis=1)
    there = scale * (over_x * over_x + over_y * over_y + GROUND * GROUND)
    one, zero = jnp.ones_like(there), jnp.zeros_like(there)
    views = jnp.concatenate(
        thirds((-2.0 * scale) * over_x) + thirds((-2.0 * scale) * over_y) + thirds(there) + [one] * 3 + [zero] * 4,
        axis=0,
    ).astype(BF16)
    width = min(128, count * listeners)
    made = []
    for left in range(0, count * listeners, width):
        view = views[:, left : left + width]
        totals = [[None] * KINDS for _ in range(HARM)]
        pending = []

        def drain(number):
            for _ in range(min(number, len(pending))):
                h, m, begin, pieces = pending.pop(0)
                whole = pieces[0] if len(pieces) == 1 else jnp.concatenate(pieces, axis=0)
                part = weights_ref[h, :, begin : begin + step]
                product = jnp.dot(part, whole, preferred_element_type=F32)
                totals[h][m] = product if totals[h][m] is None else totals[h][m] + product

        for start in range(0, owned, step):
            mats = [[[] for _ in range(KINDS)] for _ in range(HARM)]
            for row in range(start, start + step, SUB):
                square = jnp.dot(points_ref[row : row + SUB, :], view, preferred_element_type=F32)
                inv = lax.rsqrt(square)
                turns = square * inv
                frac = turns - jnp.round(turns)
                half = horner(HALF_SINE, frac * frac) * frac
                versine = half * half
                cosine = 1.0 - versine
                twoc = cosine + cosine
                rest = jnp.maximum(2.0 - versine, 1e-30)
                inv_bf = inv.astype(BF16)
                c_prev, s_prev = inv, None
                c_now = inv * cosine
                s_now = (inv * half) * (rest * lax.rsqrt(rest))
                for h in range(HARM):
                    c_bf, s_bf = c_now.astype(BF16), s_now.astype(BF16)
                    d, e = (inv * c_now).astype(BF16), (inv * s_now).astype(BF16)
                    for m, pair in enumerate(((c_bf, s_bf), (d, e), (inv_bf * d, inv_bf * e))):
                        mats[h][m].append(jnp.concatenate(pair, axis=1))
                    if h < HARM - 1:
                        c_next = twoc * c_now - c_prev
                        s_next = twoc * s_now - s_prev if h else twoc * s_now
                        c_prev, s_prev, c_now, s_now = c_now, s_now, c_next, s_next
                drain(HARM * KINDS * SUB // step)
            drain(HARM * KINDS)
            pending += [(h, m, start, mats[h][m]) for h in range(HARM) for m in range(KINDS)]
        drain(HARM * KINDS)
        ox, oy = over_x[:, left : left + width], over_y[:, left : left + width]
        rows = []
        for h in range(HARM):
            wavenum = WAVENUMBER * (h + 1)
            totals[h] = [half for both in totals[h] for half in (both[:, :width], both[:, width:])]
            cos_sum, sin_sum, d, e, u, v = totals[h]

            def loads(t):
                return ox * t[2:4] + oy * t[4:6] + (t[8:10] + t[10:12])

            plain = wavenum * sin_sum[:2] + loads((wavenum * TURN) * e + (TURN * TURN) * u)
            turned = wavenum * cos_sum[:2] + loads((wavenum * TURN) * d - (TURN * TURN) * v)
            rows.append(TURN * (plain + jnp.concatenate([-turned[1:2], turned[0:1]], axis=0)))
        made.append(jnp.concatenate(rows, axis=0))
    return made


def cells_of(lines, weights_ref, points_ref, lanes):
    listeners = lines.shape[1]
    cells = []
    for value in pair_sums(lines, weights_ref, points_ref):
        top = value.astype(BF16).astype(F32)
        split = [top, value - top]
        for j in range(value.shape[1] // listeners):
            cell = [half[:, listeners * j : listeners * j + listeners] for half in split]
            cell.append(jnp.zeros((2 * HARM, lanes - 2 * listeners), F32))
            cells.append(jnp.concatenate(cell, axis=1))
    return cells


def first_kernel(lines_ref, weights_ref, points_ref, cells_ref):
    for j, cell in enumerate(cells_of(lines_ref[...], weights_ref, points_ref, cells_ref.shape[2])):
        cells_ref[j] = cell


def second_kernel(steps, me_ref, lines_ref, weights_ref, points_ref, cells_ref, codes_ref, body_ref, packed_ref):
    nwide, rows, lanes = body_ref.shape
    for o in range(nwide):
        packed_ref[o, :rows, :] = body_ref[o]
    early = cells_ref.shape[0]
    cells = [cells_ref[j] for j in range(early)]
    cells += cells_of(lines_ref[...], weights_ref, points_ref, lanes)
    for j, cell in enumerate(cells):
        owner = me_ref[0] ^ steps[j]
        packed_ref[owner, rows:, :] = (codes_ref[owner] + cell).astype(BF16)


def first_sums(lines, weights, points, lanes):
    owned = weights.shape[2]
    devices = lines.shape[0] // 2
    pairs = devices * lines.shape[1] * owned
    vmem = pl.BlockSpec(memory_space=pltpu.VMEM)
    return pl.pallas_call(
        first_kernel,
        out_shape=jax.ShapeDtypeStruct((devices, 2 * HARM, lanes), F32),
        in_specs=[vmem] * 3,
        out_specs=vmem,
        compiler_params=pltpu.CompilerParams(vmem_limit_bytes=40 * 2**20),
        cost_estimate=pl.CostEstimate(flops=pairs * 2000, bytes_accessed=owned * 70, transcendentals=pairs),
    )(lines, weights, points)


def second_sums(lines, weights, points, cells, codes, body, steps):
    owned = weights.shape[2]
    nwide, rows, lanes = body.shape
    pairs = lines.shape[0] // 2 * lines.shape[1] * owned
    vmem = pl.BlockSpec(memory_space=pltpu.VMEM)
    me = lax.axis_index("wide").reshape(1)

    def kernel(*refs):
        second_kernel(steps, *refs)

    return pl.pallas_call(
        kernel,
        out_shape=jax.ShapeDtypeStruct((nwide, rows + 8, lanes), BF16),
        in_specs=[pl.BlockSpec(memory_space=pltpu.SMEM)] + [vmem] * 6,
        out_specs=vmem,
        compiler_params=pltpu.CompilerParams(vmem_limit_bytes=40 * 2**20),
        cost_estimate=pl.CostEstimate(flops=pairs * 2000, bytes_accessed=owned * 70, transcendentals=pairs),
    )(me, lines, weights, points, cells, codes, body)


def swap(x, nwide, bit):
    return lax.ppermute(x, "wide", [(i, i ^ bit) for i in range(nwide)])


def shards(flow, positions, normals, panel_ids, observers):
    owned = flow.shape[2]
    nwide = lax.axis_size("wide")
    listeners = observers.shape[1]
    near = nwide // 4
    others = [swap(observers, nwide, n) for n in range(1, near)]
    spectra, weights, points, ids, mine = sources(flow, normals, positions, panel_ids, observers)
    others, spectra = lax.optimization_barrier((others, spectra))
    lines = jnp.concatenate([mine] + others, axis=0)
    other = swap(lines, nwide, near)
    packed, codes = pack(spectra, ids, nwide)
    other, packed = lax.optimization_barrier((other, packed))
    lines = jnp.concatenate([lines, other], axis=0)
    other = swap(lines, nwide, 2 * near)
    cells = first_sums(lines, weights, points, packed.shape[2])
    other, cells = lax.optimization_barrier((other, cells))
    steps = [n ^ z for z in range(0, 4 * near, near) for n in range(near)]
    packed = second_sums(other, weights, points, cells, codes, packed, steps)
    received = lax.all_to_all(packed, "wide", split_axis=0, concat_axis=0, tiled=True)
    panel_spectra, pressure = place(received, owned, listeners)
    return (panel_spectra, pressure.T)


def solution(mesh):
    placed = (
        P(None, None, ("case", "wide")),
        P(None, ("case", "wide")),
        P(None, ("case", "wide")),
        P(("case", "wide")),
        P(None, ("case", "wide")),
    )
    return jax.shard_map(
        shards,
        mesh=mesh,
        in_specs=placed,
        out_specs=(P(None, ("case", "wide")), P(("case", "wide"), None)),
        check_vma=False,
    )
```
